768 devices in a mesh: grp: 12 (over z), dom: 64 (over x, y, core).
Axes of the slice: x: 4, y: 8, z: 12, core: 2. Of those that a mesh axis runs over, the one named last changes fastest.
Arguments:
- cotangent: bfloat16 [884736, 256], P(('grp', 'dom')), as said below
- features: bfloat16 [393216, 256], P(('grp', 'dom')), may hold values from -6 to 6
- aggregated: bfloat16 [393216, 256], P(('grp', 'dom')), may hold values from -6 to 6
- w_self: bfloat16 [256, 256], replicated, may hold values from -0.375 to 0.375
- w_neigh: bfloat16 [256, 256], replicated, may hold values from -0.375 to 0.375
- edge_tiles: bfloat16 [49152, 128, 128], P(('grp', 'dom')), may hold values from -0.1875 to 0.1875
- tile_rows: int32 [49152], P(('grp', 'dom')), may hold values from 0 to 8
- tile_cols: int32 [49152], P(('grp', 'dom')), may hold values from 0 to 8
- mirror_rows: int32 [768, 64, 8], P(('grp', 'dom')), may hold values from 0 to 511, as said below
- mirror_count: int32 [768, 64], P(('grp', 'dom')), may hold values from 0 to 8
- cross_rows: int32 [768, 12, 4], P(('grp', 'dom')), may hold values from 0 to 511, as said below
- cross_count: int32 [768, 12], P(('grp', 'dom')), may hold values from 0 to 4
Outputs:
- grad_slots: bfloat16 [884736, 256], P(('grp', 'dom'))
- grad_weights: float32 [2, 256, 256], replicated
The draws below stay inside these ranges and needn't reach their ends.
Inputs may be any that keep to these rules, and one draw needn't show every extreme that they name: Mirror slots of cotangent hold the row of their master when live, zeros when dead; empty slots are zero. `mirror_rows`: entries of one list are distinct; only the first mirror_count entries are live. `cross_rows`: entries of one list are distinct; only the first cross_count entries are live.
All inputs are finite; a program needn't handle non-finite values.
Results may differ from the reference program's by a relative error of at most 0.0042.
Values may be sent and summed in bfloat16 or wider, within the bound.
A program may use at most 32 MiB of HBM per device.

```python
import math
import jax
import jax.numpy as jnp
from jax import lax

F = 256
M_DEV = 512
CAP = 8
XCAP = 4
TILE = 128
K = 64
SLOTS = 1152
TILES_LOCAL = 9
VERTICES = 393216
N_GRP = 12
N_DOM = 64
DEVICES = 768


def pick_lists(base_key, peer_total, capacity):
    keys = jax.random.split(base_key, DEVICES * peer_total)
    picked = jax.vmap(lambda one_key: jax.random.permutation(one_key, M_DEV)[:capacity])(keys)
    return picked.reshape(DEVICES, peer_total, capacity).astype(jnp.int32)


def mirror_lists(key):
    mirror_rows = pick_lists(jax.random.fold_in(key, 101), N_DOM, CAP)
    cross_rows = pick_lists(jax.random.fold_in(key, 102), N_GRP, XCAP)
    level = jax.random.randint(jax.random.fold_in(key, 103), (DEVICES, 1), 1, 5)
    jitter = jax.random.randint(jax.random.fold_in(key, 104), (DEVICES, N_DOM), 0, CAP // 2 + 1) - CAP // 4
    counts = jnp.clip(level * CAP // 4 + jitter, 0, CAP)
    peer_full = jax.random.randint(jax.random.fold_in(key, 105), (DEVICES, 1), 0, N_DOM)
    columns = jnp.arange(N_DOM, dtype=jnp.int32)[None, :]
    counts = jnp.where(columns == peer_full, CAP, counts)
    column_full = jax.random.randint(jax.random.fold_in(key, 106), (N_GRP, 1, 1), 0, N_DOM)
    counts = jnp.where(columns.reshape(1, 1, N_DOM) == column_full, CAP, counts.reshape(N_GRP, N_DOM, N_DOM))
    counts = counts.reshape(DEVICES, N_DOM).astype(jnp.int32)
    cross_counts = jax.random.randint(jax.random.fold_in(key, 107), (DEVICES, N_GRP), 0, XCAP + 1)
    group_full = jax.random.randint(jax.random.fold_in(key, 108), (DEVICES, 1), 0, N_GRP)
    groups = jnp.arange(N_GRP, dtype=jnp.int32)[None, :]
    cross_counts = jnp.where(groups == group_full, XCAP, cross_counts)
    target_full = jax.random.randint(jax.random.fold_in(key, 109), (1, N_DOM, 1), 0, N_GRP)
    cross_counts = jnp.where(groups.reshape(1, 1, N_GRP) == target_full, XCAP, cross_counts.reshape(N_GRP, N_DOM, N_GRP))
    cross_counts = cross_counts.reshape(DEVICES, N_GRP).astype(jnp.int32)
    return (mirror_rows, counts, cross_rows, cross_counts)


def draw_cotangent(key, part):
    mirror_rows, counts, cross_rows, cross_counts = mirror_lists(key)
    key = jax.random.fold_in(key, 7)
    values = jax.random.normal(jax.random.fold_in(key, 2), (DEVICES, M_DEV, F), jnp.float32)
    inner_send = jax.vmap(lambda table, picks: jnp.take(table, picks, axis=0))(values, mirror_rows)
    outer_send = jax.vmap(lambda table, picks: jnp.take(table, picks, axis=0))(values, cross_rows)
    inner_live = jnp.arange(CAP, dtype=jnp.int32)[None, None, :] < counts[:, :, None]
    outer_live = jnp.arange(XCAP, dtype=jnp.int32)[None, None, :] < cross_counts[:, :, None]
    inner_send = jnp.where(inner_live[..., None], inner_send, 0.0)
    outer_send = jnp.where(outer_live[..., None], outer_send, 0.0)
    inner_copy = inner_send.reshape(N_GRP, N_DOM, N_DOM, CAP, F).transpose(0, 2, 1, 3, 4).reshape(DEVICES, N_DOM * CAP, F)
    outer_copy = outer_send.reshape(N_GRP, N_DOM, N_GRP, XCAP, F).transpose(2, 1, 0, 3, 4).reshape(DEVICES, N_GRP * XCAP, F)
    padding = jnp.zeros((DEVICES, SLOTS - M_DEV - N_DOM * CAP - N_GRP * XCAP, F), jnp.float32)
    whole = jnp.concatenate([values, inner_copy, outer_copy, padding], axis=1)
    return whole.reshape(DEVICES * SLOTS, F).astype(jnp.bfloat16)


def draw_mirror_rows(key, part):
    return mirror_lists(key)[0]


def draw_mirror_count(key, part):
    return mirror_lists(key)[1]


def draw_cross_rows(key, part):
    return mirror_lists(key)[2]


def draw_cross_count(key, part):
    return mirror_lists(key)[3]


def with_ends(values, key, smallest, largest):
    longest = values.shape.index(max(values.shape))
    spots = []
    for shift in (0, 1):
        where = [jax.random.randint(jax.random.fold_in(key, axis), (), 0, length) for axis, length in enumerate(values.shape)]
        where[longest] = (where[longest] + shift) % values.shape[longest]
        spots.append(tuple(where))
    return values.at[spots[0]].set(smallest).at[spots[1]].set(largest)


def shard_levels(rng, shape, pieces, smallest, largest):
    gain, own = 1.0, jax.random.fold_in(rng, 6)
    for axis_at, shards_of in pieces:
        heights = jnp.exp(jax.random.uniform(jax.random.fold_in(own, axis_at), (shards_of,), jnp.float32, smallest / len(pieces), largest / len(pieces)))
        gain = gain * jnp.repeat(heights, shape[axis_at] // shards_of).reshape([-1 if axis == axis_at else 1 for axis in range(len(shape))])
    return gain


def gaussian(stream_key, shape, width, bound, cuts=(), kind=jnp.bfloat16):
    array = jax.random.normal(stream_key, shape, jnp.float32) * width
    if len(cuts) > 0:
        array = shard_levels(stream_key, shape, cuts, -0.22, 0.18) * array
    return jnp.clip(array, min=-bound, max=bound).astype(kind)


def setup_inputs(seed: int = 0) -> dict:
    streams_of = jax.random.split(jax.random.key(seed), 13)
    cotangent = draw_cotangent(jax.random.fold_in(streams_of[12], 71), 0)
    features = gaussian(streams_of[1], (VERTICES, F), 1.0, 6.0, ((0, 768),))
    aggregated = gaussian(streams_of[2], (VERTICES, F), 1.0, 6.0, ((0, 768),))
    w_self = gaussian(streams_of[3], (F, F), F ** -0.5, 0.375)
    w_neigh = gaussian(streams_of[4], (F, F), F ** -0.5, 0.375)
    edge_tiles = gaussian(streams_of[5], (DEVICES * K, TILE, TILE), (TILE * K // TILES_LOCAL) ** -0.5, 0.1875, ((0, 768),))
    tile_rows = with_ends(jax.random.randint(streams_of[6], (DEVICES * K,), 0, TILES_LOCAL), jax.random.fold_in(streams_of[6], 1), 0, TILES_LOCAL - 1).astype(jnp.int32)
    tile_cols = with_ends(jax.random.randint(streams_of[7], (DEVICES * K,), 0, TILES_LOCAL), jax.random.fold_in(streams_of[7], 1), 0, TILES_LOCAL - 1).astype(jnp.int32)
    mirror_rows = draw_mirror_rows(jax.random.fold_in(streams_of[12], 71), 0)
    mirror_count = draw_mirror_count(jax.random.fold_in(streams_of[12], 71), 0)
    cross_rows = draw_cross_rows(jax.random.fold_in(streams_of[12], 71), 0)
    cross_count = draw_cross_count(jax.random.fold_in(streams_of[12], 71), 0)
    return {"cotangent": cotangent, "features": features, "aggregated": aggregated, "w_self": w_self, "w_neigh": w_neigh, "edge_tiles": edge_tiles, "tile_rows": tile_rows, "tile_cols": tile_cols, "mirror_rows": mirror_rows, "mirror_count": mirror_count, "cross_rows": cross_rows, "cross_count": cross_count}


def times_transpose(left, weight):
    return lax.dot_general(left, weight, (((1,), (1,)), ((), ())), preferred_element_type=jnp.float32)

def reference(cotangent, features, aggregated, w_self, w_neigh, edge_tiles, tile_rows, tile_cols, mirror_rows, mirror_count, cross_rows, cross_count):
    inner_end = M_DEV + N_DOM * CAP
    outer_end = inner_end + N_GRP * XCAP
    cotangent_all = cotangent.reshape(DEVICES, SLOTS, F)
    tiles_all = edge_tiles.reshape(DEVICES, K, TILE, TILE)
    rows_all = tile_rows.reshape(DEVICES, K)
    cols_all = tile_cols.reshape(DEVICES, K)

    def device_partial(inputs):
        slot_cot, tile_values, rows_in, cols_in = inputs
        neighbor_grad = times_transpose(slot_cot, w_neigh).astype(jnp.bfloat16)
        grad_blocks = neighbor_grad.reshape(TILES_LOCAL, TILE, F)
        taken_blocks = jnp.take(grad_blocks, rows_in, axis=0).astype(jnp.float32)
        product = jnp.einsum('kij,kif->kjf', tile_values.astype(jnp.float32), taken_blocks, precision=lax.Precision.HIGHEST)
        partial_value = jax.ops.segment_sum(product, cols_in, num_segments=TILES_LOCAL).reshape(SLOTS, F)
        own_term = times_transpose(slot_cot[:M_DEV], w_self) + partial_value[:M_DEV]
        return (own_term, partial_value[M_DEV:inner_end], partial_value[inner_end:outer_end])
    own_term, inner_sums, outer_sums = lax.map(device_partial, (cotangent_all, tiles_all, rows_all, cols_all))
    inner_recv = inner_sums.reshape(N_GRP, N_DOM, N_DOM, CAP, F).transpose(0, 2, 1, 3, 4).reshape(DEVICES, N_DOM, CAP, F)
    outer_recv = outer_sums.reshape(N_GRP, N_DOM, N_GRP, XCAP, F).transpose(2, 1, 0, 3, 4).reshape(DEVICES, N_GRP, XCAP, F)
    inner_live = jnp.arange(CAP, dtype=jnp.int32)[None, None, :] < mirror_count[:, :, None]
    outer_live = jnp.arange(XCAP, dtype=jnp.int32)[None, None, :] < cross_count[:, :, None]
    inner_recv = jnp.where(inner_live[..., None], inner_recv, jnp.zeros((), jnp.float32))
    outer_recv = jnp.where(outer_live[..., None], outer_recv, jnp.zeros((), jnp.float32))

    def add_mirrors(own_rows, in_rows, in_vals, out_rows, out_vals):
        summed = own_rows.at[in_rows.reshape(-1)].add(in_vals.reshape(-1, F))
        return summed.at[out_rows.reshape(-1)].add(out_vals.reshape(-1, F))
    totals = jax.vmap(add_mirrors)(own_term, mirror_rows, inner_recv, cross_rows, outer_recv)
    grad_master = totals.astype(jnp.bfloat16)
    inner_send = jax.vmap(lambda table, picks: jnp.take(table, picks, axis=0))(grad_master, mirror_rows)
    outer_send = jax.vmap(lambda table, picks: jnp.take(table, picks, axis=0))(grad_master, cross_rows)
    inner_send = jnp.where(inner_live[..., None], inner_send, jnp.zeros((), jnp.bfloat16))
    outer_send = jnp.where(outer_live[..., None], outer_send, jnp.zeros((), jnp.bfloat16))
    inner_copy = inner_send.reshape(N_GRP, N_DOM, N_DOM, CAP, F).transpose(0, 2, 1, 3, 4).reshape(DEVICES, N_DOM * CAP, F)
    outer_copy = outer_send.reshape(N_GRP, N_DOM, N_GRP, XCAP, F).transpose(2, 1, 0, 3, 4).reshape(DEVICES, N_GRP * XCAP, F)
    padding = jnp.zeros((DEVICES, SLOTS - outer_end, F), jnp.bfloat16)
    grad_slots = jnp.concatenate([grad_master, inner_copy, outer_copy, padding], axis=1).reshape(DEVICES * SLOTS, F)
    master_cot = cotangent_all[:, :M_DEV].reshape(VERTICES, F)
    joined = jnp.concatenate([features, aggregated], axis=1)
    summed = lax.dot_general(joined, master_cot, (((0,), (0,)), ((), ())), preferred_element_type=jnp.float32)
    grad_weights = (summed * (1.0 / math.sqrt(VERTICES))).reshape(2, F, F)
    return (grad_slots, grad_weights)
```

```python
import functools
import math

import jax
import jax.numpy as jnp
from jax import lax
from jax.experimental import pallas as pl
from jax.experimental.pallas import tpu as pltpu
from jax.sharding import PartitionSpec as P

F32 = jnp.float32
BF16 = jnp.bfloat16
MESH = pl.DeviceIdType.MESH
UNROLL = 8


def dot_tt(left, right):
    return lax.dot_general(left, right, (((1,), (1,)), ((), ())), preferred_element_type=F32)


def dot_nn(left, right):
    return lax.dot_general(left, right, (((1,), (0,)), ((), ())), preferred_element_type=F32)


def dot_tn(left, right):
    return lax.dot_general(left, right, (((0,), (0,)), ((), ())), preferred_element_type=F32)


def iota(shape, axis):
    return lax.broadcasted_iota(jnp.int32, shape, axis)


def one_hot(mask):
    return jnp.where(mask, 1.0, 0.0).astype(F32)


def list_lanes(rows_ref, count_ref, lanes):
    peers, capacity = rows_ref.shape[1], rows_ref.shape[2]
    entry = iota((capacity, lanes), 1) % 8
    pick = one_hot(entry == iota((capacity, lanes), 0))
    spread = lax.dot_general(
        rows_ref[0].astype(F32), pick, (((1,), (0,)), ((), ())),
        precision=lax.Precision.HIGHEST, preferred_element_type=F32,
    )
    mine = iota((peers, lanes), 1) // 8 == iota((peers, lanes), 0)
    rows = jnp.sum(jnp.where(mine, spread, 0.0), axis=0, keepdims=True)
    counts = lax.dot_general(
        count_ref[...].astype(F32), one_hot(mine), (((1,), (0,)), ((), ())),
        precision=lax.Precision.HIGHEST, preferred_element_type=F32,
    )
    live = (iota((1, lanes), 1) % 8).astype(F32) < counts
    return jnp.where(live, rows, -1.0)


def to_chunks(rows):
    count, half = rows.shape[0] // 8, rows.shape[1] // 2
    left = rows[:, :half].reshape(count, 8, half)
    right = rows[:, half:].reshape(count, 8, half)
    return jnp.concatenate([left, right], axis=1).astype(BF16)


def from_chunks(chunks):
    count, half = chunks.shape[0], chunks.shape[2]
    wide = chunks.astype(F32)
    left = wide[:, :8].reshape(count * 8, half)
    right = wide[:, 8:].reshape(count * 8, half)
    return jnp.concatenate([left, right], axis=1).astype(BF16)


def kernel(
    sizes, scale,
    cot_hbm, feat_hbm, agg_hbm, wself_hbm, wneigh_hbm, tiles_hbm,
    trow, tcol, mrow, mcnt, xrow, xcnt,
    slots_out, weights_out,
    cot, feat, agg, wself, wneigh, tiles, grads, run, part, own,
    pick, pick_t, send_a, recv_a, send_b, recv_b,
    sendx_a, recvx_a, sendx_b, recvx_b,
    w_local, w_pair, w_x, w_xin, w_z, w_zin, w_yin, w_zall, w_xall, w_other,
    load_sem, ex_sem, w_send, w_recv,
):
    nx, ny, nz, granules = sizes
    nd = nx * ny * 2
    masters = feat.shape[0]
    blocks = grads.shape[0]
    tile_total = tiles.shape[0]
    inner_end = masters + nd * 8
    z = lax.axis_index("grp")
    d = lax.axis_index("dom")
    core = d % 2
    y = (d // 2) % ny
    x = d // (2 * ny)

    def dom_of(xx, yy, cc):
        return (xx * ny + yy) * 2 + cc

    def hop(offset):
        return dom_of(
            (x + offset // (2 * ny)) % nx, (y + (offset // 2) % ny) % ny, (core + offset) % 2
        )

    loads = []
    for place, (src, dst) in enumerate(
        [(cot_hbm, cot), (feat_hbm, feat), (agg_hbm, agg), (wneigh_hbm, wneigh),
         (tiles_hbm, tiles), (wself_hbm, wself)]
    ):
        load = pltpu.make_async_copy(src, dst, load_sem.at[place])
        load.start()
        loads.append(load)

    barrier = pltpu.get_barrier_semaphore()

    @pl.loop(1, nd)
    def _(offset):
        pl.semaphore_signal(barrier, inc=1, device_id=(z, hop(offset)), device_id_type=MESH)

    @pl.loop(1, nz)
    def _(offset):
        pl.semaphore_signal(
            barrier, inc=1, device_id=((z + offset) % nz, d), device_id_type=MESH
        )

    def push(src, dst, stage, target):
        copy = pltpu.make_async_remote_copy(
            src_ref=src, dst_ref=dst, send_sem=w_send.at[stage], recv_sem=w_recv.at[stage],
            device_id=target, device_id_type=MESH,
        )
        copy.start()

    def settle(ref, sem):
        pltpu.make_async_copy(ref, ref, sem).wait()

    loads[0].wait()
    loads[1].wait()
    w_local[0] = dot_tn(feat[...], cot[:masters])
    loads[2].wait()
    w_local[1] = dot_tn(agg[...], cot[:masters])

    loads[3].wait()
    for block in range(blocks):
        rows = slice(block * 128, block * 128 + 128)
        grads[block] = dot_tt(cot[rows], wneigh[...]).astype(BF16)

    pl.semaphore_wait(barrier, nd - 1 + nz - 1)
    partner = (z, d + 1 - 2 * core)
    push(w_local.at[1 - core], w_pair, 0, partner)

    run[0] = jnp.zeros(run.shape[1:], F32)
    loads[4].wait()

    def tile_group(group, last):
        for step in range(UNROLL):
            k = group * UNROLL + step
            column = tcol[k]
            before = last[0]
            for block in range(1, blocks):
                before = jnp.where(column == block, last[block], before)
            product = dot_tn(tiles[k], grads[trow[k]])
            run[k + 1] = product + run[before]
            last = tuple(
                jnp.where(column == block, k + 1, last[block]) for block in range(blocks)
            )
        return last

    last = lax.fori_loop(
        0, tile_total // UNROLL, tile_group, tuple(jnp.int32(0) for _ in range(blocks))
    )
    for block in range(blocks):
        part[block * 128:block * 128 + 128] = run[last[block]]

    send_a[...] = to_chunks(part[masters:inner_end])
    spread = (iota((128, 128), 0) // 8 == iota((128, 128), 1) // 4) & (
        iota((128, 128), 0) % 8 == iota((128, 128), 1) % 4
    ) & (iota((128, 128), 1) < nz * 4)
    sendx_a[...] = to_chunks(
        dot_nn(one_hot(spread).astype(BF16), part[inner_end:inner_end + 128].astype(BF16))
    )

    def exchange(send, recv, sendx, recvx, stage):
        @pl.loop(1, nz)
        def _(offset):
            target = (z + offset) % nz
            pltpu.make_async_remote_copy(
                src_ref=sendx.at[target], dst_ref=recvx.at[z],
                send_sem=ex_sem.at[stage], recv_sem=ex_sem.at[stage + 1],
                device_id=(target, d), device_id_type=MESH,
            ).start()

        @pl.loop(1, nd)
        def _(offset):
            target = hop(offset)
            pltpu.make_async_remote_copy(
                src_ref=send.at[target], dst_ref=recv.at[d],
                send_sem=ex_sem.at[stage + 2], recv_sem=ex_sem.at[stage + 3],
                device_id=(z, target), device_id_type=MESH,
            ).start()

        recv[d] = send[d]
        recvx[z] = sendx[z]
        for slot in range(nz, recvx.shape[0]):
            recvx[slot] = jnp.zeros(recvx.shape[1:], BF16)

    def arrived(recv, recvx, stage):
        settle(recvx.at[pl.ds(0, nz - 1)], ex_sem.at[stage + 1])
        settle(recv.at[pl.ds(0, nd - 1)], ex_sem.at[stage + 3])

    def sent(send, sendx, stage):
        settle(sendx.at[pl.ds(0, nz - 1)], ex_sem.at[stage])
        settle(send.at[pl.ds(0, nd - 1)], ex_sem.at[stage + 2])

    exchange(send_a, recv_a, sendx_a, recvx_a, 0)

    settle(w_pair, w_recv.at[0])
    w_x[...] = (w_local[core] + w_pair[...]).reshape(w_x.shape)
    for step in range(1, nx):
        to_x = (x + step) % nx
        push(w_x.at[to_x], w_xin.at[step - 1], 1, (z, dom_of(to_x, y, core)))

    loads[5].wait()
    own[...] = dot_tt(cot[:masters], wself[...]) + part[:masters]
    inner_lanes = pick.shape[1] - 128
    lanes = jnp.concatenate(
        [list_lanes(mrow, mcnt, inner_lanes), list_lanes(xrow, xcnt, 128)], axis=1
    )
    master_of = iota(pick.shape, 0).astype(F32)
    pick[...] = one_hot(master_of == lanes).astype(BF16)

    settle(w_xin, w_recv.at[1])
    share = w_x[x]
    for step in range(nx - 1):
        share = share + w_xin[step]
    w_z[...] = share.reshape(w_z.shape)

    def owner_of(granule):
        return (granule * nz) // granules

    mine = (z * granules + nz - 1) // nz
    owner = owner_of(mine) == z

    @pl.loop(0, granules)
    def _(granule):
        target = owner_of(granule)

        @pl.when(target != z)
        def _():
            push(w_z.at[granule], w_zin.at[z], 2, (target, d))

    slots_t = jnp.transpose(jnp.broadcast_to(lanes, (128, lanes.shape[1])))
    for block in range(masters // 128):
        columns = slice(block * 128, block * 128 + 128)
        master_at = (iota(slots_t.shape, 1) + block * 128).astype(F32)
        pick_t[:, columns] = one_hot(slots_t == master_at).astype(BF16)

    @pl.when(owner)
    def _():
        w_zin[z] = w_z[mine]
        settle(w_zin.at[pl.ds(0, nz - 1)], w_recv.at[2])
        total = w_zin[0]
        for step in range(1, nz):
            total = total + w_zin[step]
        w_yin[y] = total

        @pl.loop(1, ny)
        def _(step):
            push(w_yin.at[y], w_yin.at[y], 3, (z, dom_of(x, (y + step) % ny, core)))

    arrived(recv_a, recvx_a, 0)
    back = jnp.concatenate([from_chunks(recv_a[...]), from_chunks(recvx_a[...])], axis=0)
    master = (own[...] + dot_nn(pick[...], back)).astype(BF16)
    slots_out[:masters] = master
    copies = dot_nn(pick_t[...], master)
    send_b[...] = to_chunks(copies[:inner_lanes])
    sendx_b[...] = to_chunks(copies[inner_lanes:])
    exchange(send_b, recv_b, sendx_b, recvx_b, 4)

    @pl.when(owner)
    def _():
        settle(w_yin.at[pl.ds(0, ny - 1)], w_recv.at[3])
        total = w_yin[0]
        for step in range(1, ny):
            total = total + w_yin[step]
        w_zall[mine] = total * scale

        @pl.loop(1, nz)
        def _(step):
            push(w_zall.at[mine], w_zall.at[mine], 4, ((z + step) % nz, d))

        settle(w_zall.at[pl.ds(0, granules - 1)], w_recv.at[4])

    @pl.when(jnp.logical_not(owner))
    def _():
        settle(w_zall, w_recv.at[4])

    w_xall[x] = w_zall[...].reshape(w_xall.shape[1:])
    for step in range(1, nx):
        push(w_xall.at[x], w_xall.at[x], 5, (z, dom_of((x + step) % nx, y, core)))
    settle(w_xall.at[pl.ds(0, nx - 1)], w_recv.at[5])
    push(w_xall, w_other, 6, partner)
    weights_out[core] = w_xall[...].reshape(weights_out.shape[1:])

    arrived(recv_b, recvx_b, 4)
    slots_out[masters:inner_end] = from_chunks(recv_b[...])
    gather = (iota((128, 128), 1) // 8 == iota((128, 128), 0) // 4) & (
        iota((128, 128), 1) % 8 == iota((128, 128), 0) % 4
    ) & (iota((128, 128), 0) < nz * 4)
    slots_out[inner_end:inner_end + 128] = dot_nn(
        one_hot(gather).astype(BF16), from_chunks(recvx_b[...])
    ).astype(BF16)
    tail = slots_out.shape[0] - inner_end - 128
    if tail:
        slots_out[inner_end + 128:] = jnp.zeros((tail, slots_out.shape[1]), BF16)

    settle(w_other, w_recv.at[6])
    weights_out[1 - core] = w_other[...].reshape(weights_out.shape[1:])

    sent(send_a, sendx_a, 0)
    sent(send_b, sendx_b, 4)
    settle(w_pair, w_send.at[0])
    settle(w_xin, w_send.at[1])

    @pl.when(owner)
    def _():
        settle(w_z.at[pl.ds(0, granules - 1)], w_send.at[2])
        settle(w_yin.at[pl.ds(0, ny - 1)], w_send.at[3])
        settle(w_zin.at[pl.ds(0, nz - 1)], w_send.at[4])

    @pl.when(jnp.logical_not(owner))
    def _():
        settle(w_z, w_send.at[2])

    settle(w_xall.at[pl.ds(0, nx - 1)], w_send.at[5])
    settle(w_other, w_send.at[6])


def body(
    sizes,
    cotangent, features, aggregated, w_self, w_neigh, edge_tiles,
    tile_rows, tile_cols, mirror_rows, mirror_count, cross_rows, cross_count,
):
    nx, ny, nz, granules = sizes
    nd = nx * ny * 2
    slot_count, width = cotangent.shape
    masters = features.shape[0]
    tile_total = edge_tiles.shape[0]
    blocks = slot_count // 128
    scale = 1.0 / math.sqrt(masters * nd * nz)
    share = width // nx
    grain = share // granules
    any_spec = pl.BlockSpec(memory_space=pl.ANY)
    vmem = pl.BlockSpec(memory_space=pltpu.VMEM)
    smem = pl.BlockSpec(memory_space=pltpu.SMEM)
    lanes = (nd * 8 + 127) // 128 * 128 + 128
    chunk = (16, width // 2)
    dma = pltpu.SemaphoreType.DMA
    return pl.pallas_call(
        functools.partial(kernel, sizes, scale),
        out_shape=(
            jax.ShapeDtypeStruct((slot_count, width), BF16),
            jax.ShapeDtypeStruct((2, width, width), F32),
        ),
        in_specs=[any_spec] * 6 + [smem] * 2 + [vmem] * 4,
        out_specs=(vmem, vmem),
        scratch_shapes=[
            pltpu.VMEM(cotangent.shape, BF16),
            pltpu.VMEM(features.shape, BF16),
            pltpu.VMEM(aggregated.shape, BF16),
            pltpu.VMEM(w_self.shape, BF16),
            pltpu.VMEM(w_neigh.shape, BF16),
            pltpu.VMEM(edge_tiles.shape, BF16),
            pltpu.VMEM((blocks, 128, width), BF16),
            pltpu.VMEM((tile_total + 1, 128, width), F32),
            pltpu.VMEM((slot_count, width), F32),
            pltpu.VMEM((masters, width), F32),
            pltpu.VMEM((masters, lanes), BF16),
            pltpu.VMEM((lanes, masters), BF16),
            pltpu.VMEM((nd,) + chunk, BF16),
            pltpu.VMEM((nd,) + chunk, BF16),
            pltpu.VMEM((nd,) + chunk, BF16),
            pltpu.VMEM((nd,) + chunk, BF16),
            pltpu.VMEM((16,) + chunk, BF16),
            pltpu.VMEM((16,) + chunk, BF16),
            pltpu.VMEM((16,) + chunk, BF16),
            pltpu.VMEM((16,) + chunk, BF16),
            pltpu.VMEM((2, width, width), F32),
            pltpu.VMEM((width, width), F32),
            pltpu.VMEM((nx, share, width), F32),
            pltpu.VMEM((nx - 1, share, width), F32),
            pltpu.VMEM((granules, grain, width), F32),
            pltpu.VMEM((nz, grain, width), F32),
            pltpu.VMEM((ny, grain, width), F32),
            pltpu.VMEM((granules, grain, width), F32),
            pltpu.VMEM((nx, share, width), F32),
            pltpu.VMEM((nx, share, width), F32),
            dma((6,)),
            dma((8,)),
            dma((7,)),
            dma((7,)),
        ],
        compiler_params=pltpu.CompilerParams(
            collective_id=0, has_side_effects=True, vmem_limit_bytes=48 * 1024 * 1024
        ),
    )(
        cotangent, features, aggregated, w_self, w_neigh, edge_tiles,
        tile_rows, tile_cols, mirror_rows, mirror_count, cross_rows, cross_count,
    )


def solution(mesh, grid=(4, 8)):
    nx, ny = grid
    nz = mesh.shape["grp"]
    granules = 1
    while granules * 2 <= min(nz, 256 // nx // 8):
        granules *= 2
    both = ("grp", "dom")
    placed = (
        P(both, None), P(both, None), P(both, None), P(), P(), P(both, None, None),
        P(both), P(both), P(both, None, None), P(both, None), P(both, None, None),
        P(both, None),
    )
    return jax.shard_map(
        functools.partial(body, (nx, ny, nz, granules)),
        mesh=mesh, in_specs=placed, out_specs=(P(both, None), P()), check_vma=False,
    )
```

```python
import functools
import math

import jax
import jax.numpy as jnp
from jax import lax
from jax.experimental import pallas as pl
from jax.experimental.pallas import tpu as pltpu
from jax.sharding import PartitionSpec as P

F32 = jnp.float32
BF16 = jnp.bfloat16
MESH = pl.DeviceIdType.MESH
UNROLL = 8
RS_TYPE = BF16
AG_TYPE = BF16
VMEM_LIMIT = 60 * 1024 * 1024


def dot_tt(left, right):
    return lax.dot_general(left, right, (((1,), (1,)), ((), ())), preferred_element_type=F32)


def dot_nn(left, right):
    return lax.dot_general(left, right, (((1,), (0,)), ((), ())), preferred_element_type=F32)


def dot_tn(left, right):
    return lax.dot_general(left, right, (((0,), (0,)), ((), ())), preferred_element_type=F32)


def iota(shape, axis):
    return lax.broadcasted_iota(jnp.int32, shape, axis)


def one_hot(mask):
    return jnp.where(mask, 1.0, 0.0).astype(F32)


def list_lanes(rows_ref, count_ref, lanes):
    capacity, peers = rows_ref.shape[1], rows_ref.shape[2]
    mine = iota((peers, lanes), 1) // 8 == iota((peers, lanes), 0)
    spread = lax.dot_general(
        rows_ref[0].astype(F32), one_hot(mine), (((1,), (0,)), ((), ())),
        precision=lax.Precision.HIGHEST, preferred_element_type=F32,
    )
    entry = iota((capacity, lanes), 1) % 8 == iota((capacity, lanes), 0)
    rows = jnp.sum(jnp.where(entry, spread, 0.0), axis=0, keepdims=True)
    counts = lax.dot_general(
        count_ref[...].astype(F32), one_hot(mine), (((1,), (0,)), ((), ())),
        precision=lax.Precision.HIGHEST, preferred_element_type=F32,
    )
    live = (iota((1, lanes), 1) % 8).astype(F32) < counts
    return jnp.where(live, rows, -1.0)


def to_chunks(rows, size=8):
    count, half = rows.shape[0] // size, rows.shape[1] // 2
    left = rows[:, :half].reshape(count, size, half)
    right = rows[:, half:].reshape(count, size, half)
    return jnp.concatenate([left, right], axis=1).astype(BF16)


def from_chunks(chunks):
    count, size, half = chunks.shape[0], chunks.shape[1] // 2, chunks.shape[2]
    wide = chunks.astype(F32)
    left = wide[:, :size].reshape(count * size, half)
    right = wide[:, size:].reshape(count * size, half)
    return jnp.concatenate([left, right], axis=1)


def kernel(
    sizes, scale,
    cot_hbm, feat_hbm, agg_hbm, wself_hbm, wneigh_hbm, tiles_hbm,
    trow_hbm, tcol_hbm, mrow_hbm, mcnt_hbm, xrow_hbm, xcnt_hbm,
    slots_out, weights_out,
    cot, feat, agg, wself, wneigh, tiles, trow, tcol, mrow, mcnt, xrow, xcnt, grads, run, part, own, slots,
    pick, pick_t, send_a, recv_a, send_b, recv_b,
    sendx_a, recvx_a, sendx_b, recvx_b,
    w_local, w_pair, w_rs, w_rsin, w_zin, w_ag, w_other, w_out,
    load_sem, store_sem, ex_sem, w_send, w_recv,
):
    nx, ny, nz = sizes
    nd = nx * ny * 2
    masters = feat.shape[0]
    chips = nx * ny
    grain = w_zin.shape[1]
    blocks = grads.shape[0]
    tile_total = tiles.shape[0]
    inner_end = masters + nd * 8
    z = lax.axis_index("grp")
    d = lax.axis_index("dom")
    core = d % 2
    y = (d // 2) % ny
    x = d // (2 * ny)
    chip = x * ny + y

    def away(place, length):
        return length // 2 + (place + 1) // 2 * (place % 2 * 2 - 1)

    def dom_of(xx, yy, cc):
        return (xx * ny + yy) * 2 + cc

    def hop(offset):
        return dom_of(
            (x + away(offset // 2 % nx, nx)) % nx,
            (y + away(offset // (2 * nx), ny)) % ny,
            (core + 1 - offset % 2) % 2,
        )

    def chip_hop(offset):
        return (x + away(offset % nx, nx)) % nx * ny + (y + away(offset // nx, ny)) % ny

    loads = []
    for place, (src, dst) in enumerate(
        [(cot_hbm, cot), (feat_hbm, feat), (agg_hbm, agg), (wneigh_hbm, wneigh),
         (trow_hbm, trow), (tcol_hbm, tcol), (tiles_hbm, tiles), (wself_hbm, wself),
         (mrow_hbm, mrow), (mcnt_hbm, mcnt), (xrow_hbm, xrow), (xcnt_hbm, xcnt)]
    ):
        load = pltpu.make_async_copy(src, dst, load_sem.at[place])
        load.start()
        loads.append(load)

    barrier = pltpu.get_barrier_semaphore()

    @pl.loop(0, nd - 1)
    def _(offset):
        pl.semaphore_signal(barrier, inc=1, device_id=(z, hop(offset)), device_id_type=MESH)

    @pl.loop(1, nz)
    def _(offset):
        pl.semaphore_signal(
            barrier, inc=1, device_id=((z + offset) % nz, d), device_id_type=MESH
        )

    def push(src, dst, stage, target):
        copy = pltpu.make_async_remote_copy(
            src_ref=src, dst_ref=dst, send_sem=w_send.at[stage], recv_sem=w_recv.at[stage],
            device_id=target, device_id_type=MESH,
        )
        copy.start()

    stores = []

    def store(src, dst, place):
        copy = pltpu.make_async_copy(src, dst, store_sem.at[place])
        copy.start()
        stores.append(copy)

    def settle(ref, sem):
        pltpu.make_async_copy(ref, ref, sem).wait()

    loads[0].wait()
    loads[1].wait()
    w_local[0] = dot_tn(feat[...], cot[:masters])
    loads[2].wait()
    w_local[1] = dot_tn(agg[...], cot[:masters])

    loads[3].wait()
    for block in range(blocks):
        rows = slice(block * 128, block * 128 + 128)
        grads[block] = dot_tt(cot[rows], wneigh[...]).astype(BF16)

    pl.semaphore_wait(barrier, nd - 1 + nz - 1)
    partner = (z, d + 1 - 2 * core)
    push(w_local.at[1 - core], w_pair, 0, partner)

    run[0] = jnp.zeros(run.shape[1:], F32)
    for load in loads[4:7]:
        load.wait()

    def tile_group(group, last):
        for step in range(UNROLL):
            k = group * UNROLL + step
            column = tcol[k]
            before = last[0]
            for block in range(1, blocks):
                before = jnp.where(column == block, last[block], before)
            product = dot_tn(tiles[k], grads[trow[k]])
            run[k + 1] = product + run[before]
            last = tuple(
                jnp.where(column == block, k + 1, last[block]) for block in range(blocks)
            )
        return last

    groups = tile_total // UNROLL
    last = tuple(jnp.int32(0) for _ in range(blocks))
    last = lax.fori_loop(0, groups // 2, tile_group, last)

    settle(w_pair, w_recv.at[0])
    if RS_TYPE == BF16:
        w_rs[...] = to_chunks(w_local[core] + w_pair[...], grain)
    else:
        w_rs[...] = (w_local[core] + w_pair[...]).reshape(w_rs.shape)

    @pl.loop(0, chips - 1)
    def _(offset):
        target = chip_hop(offset)
        push(w_rs.at[target], w_rsin.at[chip], 1, (z, target * 2 + core))

    w_rsin[chip] = w_rs[chip]
    last = lax.fori_loop(groups // 2, groups, tile_group, last)
    for block in range(blocks):
        part[block * 128:block * 128 + 128] = run[last[block]]

    send_a[...] = to_chunks(part[masters:inner_end])
    spread = (iota((128, 128), 0) // 8 == iota((128, 128), 1) // 4) & (
        iota((128, 128), 0) % 8 == iota((128, 128), 1) % 4
    ) & (iota((128, 128), 1) < nz * 4)
    sendx_a[...] = to_chunks(
        dot_nn(one_hot(spread).astype(BF16), part[inner_end:inner_end + 128].astype(BF16))
    )

    def exchange(send, recv, sendx, recvx, stage):
        @pl.loop(0, nd - 1)
        def _(offset):
            target = hop(offset)
            pltpu.make_async_remote_copy(
                src_ref=send.at[target], dst_ref=recv.at[d],
                send_sem=ex_sem.at[stage + 2], recv_sem=ex_sem.at[stage + 3],
                device_id=(z, target), device_id_type=MESH,
            ).start()

        @pl.loop(1, nz)
        def _(offset):
            target = (z + offset) % nz
            pltpu.make_async_remote_copy(
                src_ref=sendx.at[target], dst_ref=recvx.at[z],
                send_sem=ex_sem.at[stage], recv_sem=ex_sem.at[stage + 1],
                device_id=(target, d), device_id_type=MESH,
            ).start()

        recv[d] = send[d]
        recvx[z] = sendx[z]
        for slot in range(nz, recvx.shape[0]):
            recvx[slot] = jnp.zeros(recvx.shape[1:], BF16)

    def arrived(recv, recvx, stage):
        settle(recvx.at[pl.ds(0, nz - 1)], ex_sem.at[stage + 1])
        settle(recv.at[pl.ds(0, nd - 1)], ex_sem.at[stage + 3])

    def sent(send, sendx, stage):
        settle(sendx.at[pl.ds(0, nz - 1)], ex_sem.at[stage])
        settle(send.at[pl.ds(0, nd - 1)], ex_sem.at[stage + 2])

    exchange(send_a, recv_a, sendx_a, recvx_a, 0)

    for load in loads[7:]:
        load.wait()
    own[...] = dot_tt(cot[:masters], wself[...]) + part[:masters]
    inner_lanes = pick.shape[1] - 128
    lanes = jnp.concatenate(
        [list_lanes(mrow, mcnt, inner_lanes), list_lanes(xrow, xcnt, 128)], axis=1
    )
    master_of = iota(pick.shape, 0).astype(F32)
    pick[...] = one_hot(master_of == lanes).astype(BF16)

    slots_t = jnp.transpose(jnp.broadcast_to(lanes, (128, lanes.shape[1])))
    for block in range(masters // 128):
        columns = slice(block * 128, block * 128 + 128)
        master_at = (iota(slots_t.shape, 1) + block * 128).astype(F32)
        pick_t[:, columns] = one_hot(slots_t == master_at).astype(BF16)

    settle(w_rsin.at[pl.ds(0, chips - 1)], w_recv.at[1])
    terms = w_rsin[...]
    if RS_TYPE == BF16:
        terms = from_chunks(terms).reshape(chips, grain, w_zin.shape[2])
    w_zin[z] = jnp.sum(terms, axis=0)

    @pl.loop(0, nz - 1)
    def _(offset):
        push(w_zin.at[z], w_zin.at[z], 2, ((z + away(offset, nz)) % nz, d))

    arrived(recv_a, recvx_a, 0)
    back = jnp.concatenate([from_chunks(recv_a[...]), from_chunks(recvx_a[...])], axis=0).astype(BF16)
    master = (own[...] + dot_nn(pick[...], back)).astype(BF16)
    copies = dot_nn(pick_t[...], master)
    send_b[...] = to_chunks(copies[:inner_lanes])
    sendx_b[...] = to_chunks(copies[inner_lanes:])
    exchange(send_b, recv_b, sendx_b, recvx_b, 4)
    slots[:masters] = master
    store(slots.at[pl.ds(0, masters)], slots_out.at[pl.ds(0, masters)], 0)

    settle(w_zin.at[pl.ds(0, nz - 1)], w_recv.at[2])
    total = w_zin[0]
    for step in range(1, nz):
        total = total + w_zin[step]
    total = total * scale
    if AG_TYPE == BF16:
        total = to_chunks(total, grain)[0]
    w_ag[chip] = total

    @pl.loop(0, chips - 1)
    def _(offset):
        push(w_ag.at[chip], w_ag.at[chip], 3, (z, chip_hop(offset) * 2 + core))

    settle(w_ag.at[pl.ds(0, chips - 1)], w_recv.at[3])
    push(w_ag, w_other, 4, partner)

    def whole(part):
        return from_chunks(part[...]) if AG_TYPE == BF16 else part[...].reshape(w_out.shape[1:])

    w_out[0] = whole(w_ag)
    store(w_out.at[0], weights_out.at[core], 1)

    arrived(recv_b, recvx_b, 4)
    slots[masters:inner_end] = from_chunks(recv_b[...]).astype(BF16)
    gather = (iota((128, 128), 1) // 8 == iota((128, 128), 0) // 4) & (
        iota((128, 128), 1) % 8 == iota((128, 128), 0) % 4
    ) & (iota((128, 128), 0) < nz * 4)
    slots[inner_end:inner_end + 128] = dot_nn(
        one_hot(gather).astype(BF16), from_chunks(recvx_b[...]).astype(BF16)
    ).astype(BF16)
    tail = slots.shape[0] - inner_end - 128
    if tail:
        slots[inner_end + 128:] = jnp.zeros((tail, slots.shape[1]), BF16)
    rest = pl.ds(masters, slots.shape[0] - masters)
    store(slots.at[rest], slots_out.at[rest], 3)

    settle(w_other, w_recv.at[4])
    w_out[1] = whole(w_other)
    store(w_out.at[1], weights_out.at[1 - core], 2)

    for copy in stores:
        copy.wait()

    sent(send_a, sendx_a, 0)
    sent(send_b, sendx_b, 4)
    settle(w_pair, w_send.at[0])
    settle(w_rsin.at[pl.ds(0, chips - 1)], w_send.at[1])
    settle(w_zin.at[pl.ds(0, nz - 1)], w_send.at[2])
    settle(w_ag.at[pl.ds(0, chips - 1)], w_send.at[3])
    settle(w_other, w_send.at[4])


def hand_on(slots_in, weights_in, slots_out, weights_out, slots, weights, in_sem, out_sem):
    quarter = slots_in.shape[0] // 4
    pieces = [
        (weights_in.at[half], weights.at[half], weights_out.at[half]) for half in range(2)
    ] + [
        tuple(ref.at[pl.ds(place * quarter, quarter)] for ref in (slots_in, slots, slots_out))
        for place in range(4)
    ]
    taken = [
        pltpu.make_async_copy(src, mid, in_sem.at[place])
        for place, (src, mid, _) in enumerate(pieces)
    ]
    given = [
        pltpu.make_async_copy(mid, dst, out_sem.at[place])
        for place, (_, mid, dst) in enumerate(pieces)
    ]
    for copy in taken:
        copy.start()
    for arrived, copy in zip(taken, given):
        arrived.wait()
        copy.start()
    for copy in given:
        copy.wait()


def body(
    sizes,
    cotangent, features, aggregated, w_self, w_neigh, edge_tiles,
    tile_rows, tile_cols, mirror_rows, mirror_count, cross_rows, cross_count,
):
    nx, ny, nz = sizes
    nd = nx * ny * 2
    mirror_rows = jnp.swapaxes(mirror_rows, 1, 2)
    cross_rows = jnp.swapaxes(cross_rows, 1, 2)
    slot_count, width = cotangent.shape
    masters = features.shape[0]
    tile_total = edge_tiles.shape[0]
    blocks = slot_count // 128
    scale = 1.0 / math.sqrt(masters * nd * nz)
    grain = width // (nx * ny)
    wide = (nx * ny, grain, width)
    narrow = (nx * ny, 2 * grain, width // 2)
    rs_shape = narrow if RS_TYPE == BF16 else wide
    ag_shape = narrow if AG_TYPE == BF16 else wide
    hbm = pl.BlockSpec(memory_space=pltpu.HBM)
    lanes = (nd * 8 + 127) // 128 * 128 + 128
    chunk = (16, width // 2)
    dma = pltpu.SemaphoreType.DMA
    outs = (
        jax.ShapeDtypeStruct((slot_count, width), BF16),
        jax.ShapeDtypeStruct((2, width, width), F32),
    )
    found = pl.pallas_call(
        functools.partial(kernel, sizes, scale),
        out_shape=outs,
        in_specs=[hbm] * 12,
        out_specs=(hbm, hbm),
        scratch_shapes=[
            pltpu.VMEM(cotangent.shape, BF16),
            pltpu.VMEM(features.shape, BF16),
            pltpu.VMEM(aggregated.shape, BF16),
            pltpu.VMEM(w_self.shape, BF16),
            pltpu.VMEM(w_neigh.shape, BF16),
            pltpu.VMEM(edge_tiles.shape, BF16),
            pltpu.SMEM(tile_rows.shape, jnp.int32),
            pltpu.SMEM(tile_cols.shape, jnp.int32),
            pltpu.VMEM(mirror_rows.shape, jnp.int32),
            pltpu.VMEM(mirror_count.shape, jnp.int32),
            pltpu.VMEM(cross_rows.shape, jnp.int32),
            pltpu.VMEM(cross_count.shape, jnp.int32),
            pltpu.VMEM((blocks, 128, width), BF16),
            pltpu.VMEM((tile_total + 1, 128, width), F32),
            pltpu.VMEM((slot_count, width), F32),
            pltpu.VMEM((masters, width), F32),
            pltpu.VMEM((slot_count, width), BF16),
            pltpu.VMEM((masters, lanes), BF16),
            pltpu.VMEM((lanes, masters), BF16),
            pltpu.VMEM((nd,) + chunk, BF16),
            pltpu.VMEM((nd,) + chunk, BF16),
            pltpu.VMEM((nd,) + chunk, BF16),
            pltpu.VMEM((nd,) + chunk, BF16),
            pltpu.VMEM((16,) + chunk, BF16),
            pltpu.VMEM((16,) + chunk, BF16),
            pltpu.VMEM((16,) + chunk, BF16),
            pltpu.VMEM((16,) + chunk, BF16),
            pltpu.VMEM((2, width, width), F32),
            pltpu.VMEM((width, width), F32),
            pltpu.VMEM(rs_shape, RS_TYPE),
            pltpu.VMEM(rs_shape, RS_TYPE),
            pltpu.VMEM((nz, grain, width), F32),
            pltpu.VMEM(ag_shape, AG_TYPE),
            pltpu.VMEM(ag_shape, AG_TYPE),
            pltpu.VMEM((2, width, width), F32),
            dma((12,)),
            dma((4,)),
            dma((8,)),
            dma((5,)),
            dma((5,)),
        ],
        compiler_params=pltpu.CompilerParams(
            collective_id=0, has_side_effects=True, vmem_limit_bytes=VMEM_LIMIT
        ),
    )(
        cotangent, features, aggregated, w_self, w_neigh, edge_tiles,
        tile_rows, tile_cols, mirror_rows, mirror_count, cross_rows, cross_count,
    )
    return pl.pallas_call(
        hand_on,
        out_shape=outs,
        in_specs=[hbm, hbm],
        out_specs=(hbm, hbm),
        scratch_shapes=[
            pltpu.VMEM(outs[0].shape, BF16), pltpu.VMEM(outs[1].shape, F32), dma((6,)), dma((6,)),
        ],
        compiler_params=pltpu.CompilerParams(vmem_limit_bytes=VMEM_LIMIT),
    )(*found)


def solution(mesh, grid=(4, 8)):
    nx, ny = grid
    nz = mesh.shape["grp"]
    both = ("grp", "dom")
    placed = (
        P(both, None), P(both, None), P(both, None), P(), P(), P(both, None, None),
        P(both), P(both), P(both, None, None), P(both, None), P(both, None, None),
        P(both, None),
    )
    return jax.shard_map(
        functools.partial(body, (nx, ny, nz)),
        mesh=mesh, in_specs=placed, out_specs=(P(both, None), P()), check_vma=False,
    )
```

```python
import functools
import math

import jax
import jax.numpy as jnp
from jax import lax
from jax.experimental import pallas as pl
from jax.experimental.pallas import tpu as pltpu
from jax.sharding import PartitionSpec as P

F32 = jnp.float32
BF16 = jnp.bfloat16
MESH = pl.DeviceIdType.MESH
UNROLL = 8
Z_TYPE = F32
VMEM_LIMIT = 60 * 1024 * 1024


def dot_tt(left, right):
    return lax.dot_general(left, right, (((1,), (1,)), ((), ())), preferred_element_type=F32)


def dot_nn(left, right):
    return lax.dot_general(left, right, (((1,), (0,)), ((), ())), preferred_element_type=F32)


def dot_tn(left, right):
    return lax.dot_general(left, right, (((0,), (0,)), ((), ())), preferred_element_type=F32)


def iota(shape, axis):
    return lax.broadcasted_iota(jnp.int32, shape, axis)


def one_hot(mask):
    return jnp.where(mask, 1.0, 0.0).astype(F32)


def list_lanes(rows_ref, count_ref, lanes):
    capacity, peers = rows_ref.shape[1], rows_ref.shape[2]
    mine = iota((peers, lanes), 1) // 8 == iota((peers, lanes), 0)
    spread = lax.dot_general(
        rows_ref[0].astype(F32), one_hot(mine), (((1,), (0,)), ((), ())),
        precision=lax.Precision.HIGHEST, preferred_element_type=F32,
    )
    entry = iota((capacity, lanes), 1) % 8 == iota((capacity, lanes), 0)
    rows = jnp.sum(jnp.where(entry, spread, 0.0), axis=0, keepdims=True)
    counts = lax.dot_general(
        count_ref[...].astype(F32), one_hot(mine), (((1,), (0,)), ((), ())),
        precision=lax.Precision.HIGHEST, preferred_element_type=F32,
    )
    live = (iota((1, lanes), 1) % 8).astype(F32) < counts
    return jnp.where(live, rows, -1.0)


def to_chunks(rows, size=8):
    count, half = rows.shape[0] // size, rows.shape[1] // 2
    left = rows[:, :half].reshape(count, size, half)
    right = rows[:, half:].reshape(count, size, half)
    return jnp.concatenate([left, right], axis=1).astype(BF16)


def from_chunks(chunks):
    count, size, half = chunks.shape[0], chunks.shape[1] // 2, chunks.shape[2]
    wide = chunks.astype(F32)
    left = wide[:, :size].reshape(count * size, half)
    right = wide[:, size:].reshape(count * size, half)
    return jnp.concatenate([left, right], axis=1)


def kernel(
    sizes, scale,
    cot_hbm, feat_hbm, agg_hbm, wself_hbm, wneigh_hbm, tiles_hbm,
    trow_hbm, tcol_hbm, mrow_hbm, mcnt_hbm, xrow_hbm, xcnt_hbm,
    master_out, recv_b, recvx_b, w_out,
    cot, feat, agg, wself, wneigh, tiles, trow, tcol, mrow, mcnt, xrow, xcnt, grads, run, part, own, master,
    pick, pick_t, send_a, recv_a, send_b, sendx_a, recvx_a, sendx_b,
    w_local, w_pair, w_rs, w_rsin, w_zin, w_ag,
    load_sem, store_sem, ex_sem, w_send, w_recv,
):
    nx, ny, nz = sizes
    nd = nx * ny * 2
    masters = feat.shape[0]
    chips = nx * ny
    grain = w_zin.shape[1] // 2
    blocks = grads.shape[0]
    tile_total = tiles.shape[0]
    inner_end = masters + nd * 8
    z = lax.axis_index("grp")
    d = lax.axis_index("dom")
    core = d % 2
    y = (d // 2) % ny
    x = d // (2 * ny)
    chip = x * ny + y

    def away(place, length):
        return length // 2 + (place + 1) // 2 * (place % 2 * 2 - 1)

    def dom_of(xx, yy, cc):
        return (xx * ny + yy) * 2 + cc

    def hop(offset):
        return dom_of(
            (x + away(offset // 2 % nx, nx)) % nx,
            (y + away(offset // (2 * nx), ny)) % ny,
            (core + 1 - offset % 2) % 2,
        )

    def chip_hop(offset):
        return (x + away(offset % nx, nx)) % nx * ny + (y + away(offset // nx, ny)) % ny

    loads = []
    for place, (src, dst) in enumerate(
        [(cot_hbm, cot), (wneigh_hbm, wneigh), (trow_hbm, trow), (tcol_hbm, tcol),
         (tiles_hbm, tiles), (feat_hbm, feat), (agg_hbm, agg), (wself_hbm, wself),
         (mrow_hbm, mrow), (mcnt_hbm, mcnt), (xrow_hbm, xrow), (xcnt_hbm, xcnt)]
    ):
        load = pltpu.make_async_copy(src, dst, load_sem.at[place])
        load.start()
        loads.append(load)

    barrier = pltpu.get_barrier_semaphore()

    @pl.loop(0, nd - 1)
    def _(offset):
        pl.semaphore_signal(barrier, inc=1, device_id=(z, hop(offset)), device_id_type=MESH)

    @pl.loop(1, nz)
    def _(offset):
        pl.semaphore_signal(
            barrier, inc=1, device_id=((z + offset) % nz, d), device_id_type=MESH
        )

    def push(src, dst, stage, target):
        copy = pltpu.make_async_remote_copy(
            src_ref=src, dst_ref=dst, send_sem=w_send.at[stage], recv_sem=w_recv.at[stage],
            device_id=target, device_id_type=MESH,
        )
        copy.start()

    stores = []

    def store(src, dst, place):
        copy = pltpu.make_async_copy(src, dst, store_sem.at[place])
        copy.start()
        stores.append(copy)

    def settle(ref, sem):
        pltpu.make_async_copy(ref, ref, sem).wait()

    loads[0].wait()
    loads[1].wait()
    for block in range(blocks):
        rows = slice(block * 128, block * 128 + 128)
        grads[block] = dot_tt(cot[rows], wneigh[...]).astype(BF16)

    run[0] = jnp.zeros(run.shape[1:], F32)
    for load in loads[2:5]:
        load.wait()

    def tile_group(group, last):
        for step in range(UNROLL):
            k = group * UNROLL + step
            column = tcol[k]
            before = last[0]
            for block in range(1, blocks):
                before = jnp.where(column == block, last[block], before)
            product = dot_tn(tiles[k], grads[trow[k]])
            run[k + 1] = product + run[before]
            last = tuple(
                jnp.where(column == block, k + 1, last[block]) for block in range(blocks)
            )
        return last

    groups = tile_total // UNROLL
    last = tuple(jnp.int32(0) for _ in range(blocks))
    last = lax.fori_loop(0, groups // 2, tile_group, last)

    loads[5].wait()
    w_local[0] = dot_tn(feat[...], cot[:masters])
    loads[6].wait()
    w_local[1] = dot_tn(agg[...], cot[:masters])

    pl.semaphore_wait(barrier, nd - 1 + nz - 1)
    partner = (z, d + 1 - 2 * core)
    push(w_local.at[1 - core], w_pair, 0, partner)

    last = lax.fori_loop(groups // 2, groups, tile_group, last)
    for block in range(blocks):
        part[block * 128:block * 128 + 128] = run[last[block]]


    settle(w_pair, w_recv.at[0])
    w_rs[...] = to_chunks(w_local[core] + w_pair[...], grain)

    @pl.loop(0, chips - 1)
    def _(offset):
        target = chip_hop(offset)
        push(w_rs.at[target], w_rsin.at[chip], 1, (z, target * 2 + core))

    w_rsin[chip] = w_rs[chip]
    send_a[...] = to_chunks(part[masters:inner_end])
    spread = (iota((128, 128), 0) // 8 == iota((128, 128), 1) // 4) & (
        iota((128, 128), 0) % 8 == iota((128, 128), 1) % 4
    ) & (iota((128, 128), 1) < nz * 4)
    sendx_a[...] = to_chunks(
        dot_nn(one_hot(spread).astype(BF16), part[inner_end:inner_end + 128].astype(BF16))
    )

    def exchange(send, recv, sendx, recvx, stage):
        @pl.loop(0, nd - 1)
        def _(offset):
            target = hop(offset)
            pltpu.make_async_remote_copy(
                src_ref=send.at[target], dst_ref=recv.at[d],
                send_sem=ex_sem.at[stage + 2], recv_sem=ex_sem.at[stage + 3],
                device_id=(z, target), device_id_type=MESH,
            ).start()

        @pl.loop(1, nz)
        def _(offset):
            target = (z + offset) % nz
            pltpu.make_async_remote_copy(
                src_ref=sendx.at[target], dst_ref=recvx.at[z],
                send_sem=ex_sem.at[stage], recv_sem=ex_sem.at[stage + 1],
                device_id=(target, d), device_id_type=MESH,
            ).start()

    def arrived(recv, recvx, stage):
        settle(recvx.at[pl.ds(0, nz - 1)], ex_sem.at[stage + 1])
        settle(recv.at[pl.ds(0, nd - 1)], ex_sem.at[stage + 3])

    def sent(send, sendx, stage):
        settle(sendx.at[pl.ds(0, nz - 1)], ex_sem.at[stage])
        settle(send.at[pl.ds(0, nd - 1)], ex_sem.at[stage + 2])

    exchange(send_a, recv_a, sendx_a, recvx_a, 0)
    recv_a[d] = send_a[d]
    recvx_a[z] = sendx_a[z]
    for slot in range(nz, recvx_a.shape[0]):
        recvx_a[slot] = jnp.zeros(recvx_a.shape[1:], BF16)

    for load in loads[7:]:
        load.wait()
    own[...] = dot_tt(cot[:masters], wself[...]) + part[:masters]
    inner_lanes = pick.shape[1] - 128
    lanes = jnp.concatenate(
        [list_lanes(mrow, mcnt, inner_lanes), list_lanes(xrow, xcnt, 128)], axis=1
    )
    master_of = iota(pick.shape, 0).astype(F32)
    pick[...] = one_hot(master_of == lanes).astype(BF16)

    slots_t = jnp.transpose(jnp.broadcast_to(lanes, (128, lanes.shape[1])))
    for block in range(masters // 128):
        columns = slice(block * 128, block * 128 + 128)
        master_at = (iota(slots_t.shape, 1) + block * 128).astype(F32)
        pick_t[:, columns] = one_hot(slots_t == master_at).astype(BF16)

    settle(w_rsin.at[pl.ds(0, chips - 1)], w_recv.at[1])
    w_zin[z] = jnp.sum(w_rsin[...].astype(F32), axis=0).astype(Z_TYPE)

    @pl.loop(0, nz - 1)
    def _(offset):
        push(w_zin.at[z], w_zin.at[z], 2, ((z + away(offset, nz)) % nz, d))

    arrived(recv_a, recvx_a, 0)
    back = jnp.concatenate([from_chunks(recv_a[...]), from_chunks(recvx_a[...])], axis=0).astype(BF16)
    master[...] = (own[...] + dot_nn(pick[...], back)).astype(BF16)
    copies = dot_nn(pick_t[...], master[...])
    send_b[...] = to_chunks(copies[:inner_lanes])
    sendx_b[...] = to_chunks(copies[inner_lanes:])
    settle(w_zin.at[pl.ds(0, nz - 1)], w_recv.at[2])
    total = w_zin[0].astype(F32)
    for step in range(1, nz):
        total = total + w_zin[step].astype(F32)
    w_ag[chip] = (total * scale).astype(BF16)

    @pl.loop(0, chips - 1)
    def _(offset):
        push(w_ag.at[chip], w_ag.at[chip], 3, (z, chip_hop(offset) * 2 + core))

    exchange(send_b, recv_b, sendx_b, recvx_b, 4)
    store(master, master_out, 0)
    store(send_b.at[d], recv_b.at[d], 1)
    store(sendx_b.at[z], recvx_b.at[z], 2)

    settle(w_ag.at[pl.ds(0, chips - 1)], w_recv.at[3])
    push(w_ag, w_out.at[core], 4, partner)
    store(w_ag, w_out.at[core], 3)

    arrived(recv_b, recvx_b, 4)
    settle(w_ag, w_recv.at[4])
    for copy in stores:
        copy.wait()

    sent(send_a, sendx_a, 0)
    sent(send_b, sendx_b, 4)
    settle(w_pair, w_send.at[0])
    settle(w_rsin.at[pl.ds(0, chips - 1)], w_send.at[1])
    settle(w_zin.at[pl.ds(0, nz - 1)], w_send.at[2])
    settle(w_ag.at[pl.ds(0, chips - 1)], w_send.at[3])
    settle(w_ag, w_send.at[4])


def finish(
    nz, master_in, recv_in, recvx_in, w_in, slots_out, weights_out,
    master, recv, recvx, parts, slots, weights, in_sem, out_sem,
):
    taken = [
        pltpu.make_async_copy(src, dst, in_sem.at[place])
        for place, (src, dst) in enumerate(
            [(w_in, parts), (recv_in, recv), (master_in, master), (recvx_in, recvx)]
        )
    ]
    for copy in taken:
        copy.start()
    masters, inner = master.shape[0], recv.shape[0] * 8
    inner_end = masters + inner
    given = []

    def give(src, dst):
        copy = pltpu.make_async_copy(src, dst, out_sem.at[len(given)])
        copy.start()
        given.append(copy)

    taken[0].wait()
    for half in range(2):
        weights[half] = from_chunks(parts[half])
        give(weights.at[half], weights_out.at[half])
    taken[1].wait()
    slots[:inner] = from_chunks(recv[...]).astype(BF16)
    give(slots.at[pl.ds(0, inner)], slots_out.at[pl.ds(masters, inner)])
    taken[2].wait()
    give(master, slots_out.at[pl.ds(0, masters)])
    taken[3].wait()
    lists = from_chunks(recvx[...]).astype(BF16)
    tail = slots.shape[0] - inner
    row, column = iota((tail, nz * 8), 0), iota((tail, nz * 8), 1)
    gather = (column // 8 == row // 4) & (column % 8 == row % 4) & (row < nz * 4)
    slots[inner:] = dot_nn(one_hot(gather).astype(BF16), lists).astype(BF16)
    give(slots.at[pl.ds(inner, tail)], slots_out.at[pl.ds(inner_end, tail)])
    for copy in given:
        copy.wait()


def body(
    sizes,
    cotangent, features, aggregated, w_self, w_neigh, edge_tiles,
    tile_rows, tile_cols, mirror_rows, mirror_count, cross_rows, cross_count,
):
    nx, ny, nz = sizes
    nd = nx * ny * 2
    mirror_rows = jnp.swapaxes(mirror_rows, 1, 2)
    cross_rows = jnp.swapaxes(cross_rows, 1, 2)
    slot_count, width = cotangent.shape
    masters = features.shape[0]
    tile_total = edge_tiles.shape[0]
    blocks = slot_count // 128
    scale = 1.0 / math.sqrt(masters * nd * nz)
    grain = width // (nx * ny)
    narrow = (nx * ny, 2 * grain, width // 2)
    hbm = pl.BlockSpec(memory_space=pltpu.HBM)
    lanes = (nd * 8 + 127) // 128 * 128 + 128
    chunk = (16, width // 2)
    dma = pltpu.SemaphoreType.DMA
    outs = (
        jax.ShapeDtypeStruct((slot_count, width), BF16),
        jax.ShapeDtypeStruct((2, width, width), F32),
    )
    landed = (
        jax.ShapeDtypeStruct((masters, width), BF16),
        jax.ShapeDtypeStruct((nd,) + chunk, BF16),
        jax.ShapeDtypeStruct((nz,) + chunk, BF16),
        jax.ShapeDtypeStruct((2,) + narrow, BF16),
    )
    found = pl.pallas_call(
        functools.partial(kernel, sizes, scale),
        out_shape=landed,
        in_specs=[hbm] * 12,
        out_specs=(hbm,) * 4,
        scratch_shapes=[
            pltpu.VMEM(cotangent.shape, BF16),
            pltpu.VMEM(features.shape, BF16),
            pltpu.VMEM(aggregated.shape, BF16),
            pltpu.VMEM(w_self.shape, BF16),
            pltpu.VMEM(w_neigh.shape, BF16),
            pltpu.VMEM(edge_tiles.shape, BF16),
            pltpu.SMEM(tile_rows.shape, jnp.int32),
            pltpu.SMEM(tile_cols.shape, jnp.int32),
            pltpu.VMEM(mirror_rows.shape, jnp.int32),
            pltpu.VMEM(mirror_count.shape, jnp.int32),
            pltpu.VMEM(cross_rows.shape, jnp.int32),
            pltpu.VMEM(cross_count.shape, jnp.int32),
            pltpu.VMEM((blocks, 128, width), BF16),
            pltpu.VMEM((tile_total + 1, 128, width), F32),
            pltpu.VMEM((slot_count, width), F32),
            pltpu.VMEM((masters, width), F32),
            pltpu.VMEM((masters, width), BF16),
            pltpu.VMEM((masters, lanes), BF16),
            pltpu.VMEM((lanes, masters), BF16),
            pltpu.VMEM((nd,) + chunk, BF16),
            pltpu.VMEM((nd,) + chunk, BF16),
            pltpu.VMEM((nd,) + chunk, BF16),
            pltpu.VMEM((16,) + chunk, BF16),
            pltpu.VMEM((16,) + chunk, BF16),
            pltpu.VMEM((16,) + chunk, BF16),
            pltpu.VMEM((2, width, width), F32),
            pltpu.VMEM((width, width), F32),
            pltpu.VMEM(narrow, BF16),
            pltpu.VMEM(narrow, BF16),
            pltpu.VMEM((nz,) + narrow[1:], Z_TYPE),
            pltpu.VMEM(narrow, BF16),
            dma((12,)),
            dma((4,)),
            dma((8,)),
            dma((5,)),
            dma((5,)),
        ],
        compiler_params=pltpu.CompilerParams(
            collective_id=0, has_side_effects=True, vmem_limit_bytes=VMEM_LIMIT
        ),
    )(
        cotangent, features, aggregated, w_self, w_neigh, edge_tiles,
        tile_rows, tile_cols, mirror_rows, mirror_count, cross_rows, cross_count,
    )
    return pl.pallas_call(
        functools.partial(finish, nz),
        out_shape=outs,
        in_specs=[hbm] * 4,
        out_specs=(hbm, hbm),
        scratch_shapes=[pltpu.VMEM(array.shape, array.dtype) for array in landed]
        + [
            pltpu.VMEM((slot_count - masters, width), BF16),
            pltpu.VMEM(outs[1].shape, F32),
            dma((4,)),
            dma((5,)),
        ],
        compiler_params=pltpu.CompilerParams(vmem_limit_bytes=VMEM_LIMIT),
    )(*found)


def solution(mesh, grid=(4, 8)):
    nx, ny = grid
    nz = mesh.shape["grp"]
    both = ("grp", "dom")
    placed = (
        P(both, None), P(both, None), P(both, None), P(), P(), P(both, None, None),
        P(both), P(both), P(both, None, None), P(both, None), P(both, None, None),
        P(both, None),
    )
    return jax.shard_map(
        functools.partial(body, (nx, ny, nz)),
        mesh=mesh, in_specs=placed, out_specs=(P(both, None), P()), check_vma=False,
    )
```

```python
import functools
import math

import jax
import jax.numpy as jnp
from jax import lax
from jax.experimental import pallas as pl
from jax.experimental.pallas import tpu as pltpu
from jax.sharding import PartitionSpec as P

F32 = jnp.float32
BF16 = jnp.bfloat16
MESH = pl.DeviceIdType.MESH
UNROLL = 8
Z_TYPE = F32
VMEM_LIMIT = 60 * 1024 * 1024


def dot_tt(left, right):
    return lax.dot_general(left, right, (((1,), (1,)), ((), ())), preferred_element_type=F32)


def dot_nn(left, right):
    return lax.dot_general(left, right, (((1,), (0,)), ((), ())), preferred_element_type=F32)


def dot_tn(left, right):
    return lax.dot_general(left, right, (((0,), (0,)), ((), ())), preferred_element_type=F32)


def iota(shape, axis):
    return lax.broadcasted_iota(jnp.int32, shape, axis)


def one_hot(mask):
    return jnp.where(mask, 1.0, 0.0).astype(F32)


def list_lanes(rows_ref, count_ref, lanes):
    capacity, peers = rows_ref.shape[1], rows_ref.shape[2]
    mine = iota((peers, lanes), 1) // 8 == iota((peers, lanes), 0)
    spread = lax.dot_general(
        rows_ref[0].astype(F32), one_hot(mine), (((1,), (0,)), ((), ())),
        precision=lax.Precision.HIGHEST, preferred_element_type=F32,
    )
    entry = iota((capacity, lanes), 1) % 8 == iota((capacity, lanes), 0)
    rows = jnp.sum(jnp.where(entry, spread, 0.0), axis=0, keepdims=True)
    counts = lax.dot_general(
        count_ref[...].astype(F32), one_hot(mine), (((1,), (0,)), ((), ())),
        precision=lax.Precision.HIGHEST, preferred_element_type=F32,
    )
    live = (iota((1, lanes), 1) % 8).astype(F32) < counts
    return jnp.where(live, rows, -1.0)


def to_chunks(rows, size=8):
    count, half = rows.shape[0] // size, rows.shape[1] // 2
    left = rows[:, :half].reshape(count, size, half)
    right = rows[:, half:].reshape(count, size, half)
    return jnp.concatenate([left, right], axis=1).astype(BF16)


def from_chunks(chunks):
    count, size, half = chunks.shape[0], chunks.shape[1] // 2, chunks.shape[2]
    wide = chunks.astype(F32)
    left = wide[:, :size].reshape(count * size, half)
    right = wide[:, size:].reshape(count * size, half)
    return jnp.concatenate([left, right], axis=1)


def kernel(
    sizes, scale,
    cot_hbm, feat_hbm, agg_hbm, wself_hbm, wneigh_hbm, tiles_hbm,
    trow_hbm, tcol_hbm, mrow_hbm, mcnt_hbm, xrow_hbm, xcnt_hbm,
    master_out, recv_b, recvx_b, w_out,
    cot, feat, agg, wself, wneigh, tiles, trow, tcol, mrow, mcnt, xrow, xcnt, grads, run, part, own, master,
    pick, pick_t, send_a, recv_a, send_b, sendx_a, recvx_a, sendx_b,
    w_local, w_pair, w_rs, w_rsin, w_zin, w_ag,
    load_sem, store_sem, ex_sem, w_send, w_recv,
):
    nx, ny, nz = sizes
    nd = nx * ny * 2
    masters = feat.shape[0]
    chips = nx * ny
    grain = w_zin.shape[1] // 2
    blocks = grads.shape[0]
    tile_total = tiles.shape[0]
    inner_end = masters + nd * 8
    z = lax.axis_index("grp")
    d = lax.axis_index("dom")
    core = lax.rem(d, 2)
    y = lax.rem(lax.div(d, 2), ny)
    x = lax.div(d, 2 * ny)
    chip = x * ny + y

    def away(place, length):
        return length // 2 + (place + 1) // 2 * (place % 2 * 2 - 1)

    x_ahead = [lax.rem(x + away(step, nx), nx) * ny for step in range(nx)]

    def each_chip(act, with_cores):
        def column(y_there, last):
            for step in range(nx):
                there = (x_ahead[step] + y_there) * 2
                own = last and step == nx - 1
                if with_cores:
                    act(there + 1 - core)
                if not own:
                    act(there + core)

        @pl.loop(0, ny - 1)
        def _(step):
            column(lax.rem(y + away(step, ny), ny), False)

        column(y, True)

    def each_z(act):
        for step in range(nz - 1):
            act(lax.rem(z + away(step, nz), nz))

    barrier = pltpu.get_barrier_semaphore()

    def greet(target):
        pl.semaphore_signal(barrier, inc=1, device_id=target, device_id_type=MESH)

    each_z(lambda there: greet((there, d)))

    loads = []
    for place, (src, dst) in enumerate(
        [(cot_hbm, cot), (wneigh_hbm, wneigh), (trow_hbm, trow), (tcol_hbm, tcol),
         (tiles_hbm, tiles), (feat_hbm, feat), (agg_hbm, agg), (wself_hbm, wself),
         (mrow_hbm, mrow), (mcnt_hbm, mcnt), (xrow_hbm, xrow), (xcnt_hbm, xcnt)]
    ):
        load = pltpu.make_async_copy(src, dst, load_sem.at[place])
        load.start()
        loads.append(load)

    each_chip(lambda there: greet((z, there)), True)

    def push(src, dst, stage, target):
        copy = pltpu.make_async_remote_copy(
            src_ref=src, dst_ref=dst, send_sem=w_send.at[stage], recv_sem=w_recv.at[stage],
            device_id=target, device_id_type=MESH,
        )
        copy.start()

    stores = []

    def store(src, dst, place):
        copy = pltpu.make_async_copy(src, dst, store_sem.at[place])
        copy.start()
        stores.append(copy)

    def settle(ref, sem):
        pltpu.make_async_copy(ref, ref, sem).wait()

    loads[0].wait()
    loads[1].wait()
    for block in range(blocks):
        rows = slice(block * 128, block * 128 + 128)
        grads[block] = dot_tt(cot[rows], wneigh[...]).astype(BF16)

    run[0] = jnp.zeros(run.shape[1:], F32)
    for load in loads[2:5]:
        load.wait()

    def tile_group(group, last):
        for step in range(UNROLL):
            k = group * UNROLL + step
            column = tcol[k]
            before = last[0]
            for block in range(1, blocks):
                before = jnp.where(column == block, last[block], before)
            product = dot_tn(tiles[k], grads[trow[k]])
            run[k + 1] = product + run[before]
            last = tuple(
                jnp.where(column == block, k + 1, last[block]) for block in range(blocks)
            )
        return last

    groups = tile_total // UNROLL
    last = tuple(jnp.int32(0) for _ in range(blocks))
    last = lax.fori_loop(0, groups // 2, tile_group, last)

    loads[5].wait()
    w_local[0] = dot_tn(feat[...], cot[:masters])
    loads[6].wait()
    w_local[1] = dot_tn(agg[...], cot[:masters])

    pl.semaphore_wait(barrier, nd - 1 + nz - 1)
    partner = (z, d + 1 - 2 * core)
    push(w_local.at[1 - core], w_pair, 0, partner)

    last = lax.fori_loop(groups // 2, groups, tile_group, last)
    for block in range(blocks):
        part[block * 128:block * 128 + 128] = run[last[block]]


    send_a[...] = to_chunks(part[masters:inner_end])
    spread = (iota((128, 128), 0) // 8 == iota((128, 128), 1) // 4) & (
        iota((128, 128), 0) % 8 == iota((128, 128), 1) % 4
    ) & (iota((128, 128), 1) < nz * 4)
    sendx_a[...] = to_chunks(
        dot_nn(one_hot(spread).astype(BF16), part[inner_end:inner_end + 128].astype(BF16))
    )

    settle(w_pair, w_recv.at[0])
    w_rs[...] = to_chunks(w_local[core] + w_pair[...], grain)

    each_chip(
        lambda there: push(w_rs.at[lax.div(there, 2)], w_rsin.at[chip], 1, (z, there)), False
    )

    w_rsin[chip] = w_rs[chip]
    def exchange(send, recv, sendx, recvx, stage):
        def to_peer(target):
            pltpu.make_async_remote_copy(
                src_ref=send.at[target], dst_ref=recv.at[d],
                send_sem=ex_sem.at[stage + 2], recv_sem=ex_sem.at[stage + 3],
                device_id=(z, target), device_id_type=MESH,
            ).start()

        def to_group(target):
            pltpu.make_async_remote_copy(
                src_ref=sendx.at[target], dst_ref=recvx.at[z],
                send_sem=ex_sem.at[stage], recv_sem=ex_sem.at[stage + 1],
                device_id=(target, d), device_id_type=MESH,
            ).start()

        each_chip(to_peer, True)
        each_z(to_group)

    def arrived(recv, recvx, stage):
        settle(recvx.at[pl.ds(0, nz - 1)], ex_sem.at[stage + 1])
        settle(recv.at[pl.ds(0, nd - 1)], ex_sem.at[stage + 3])

    def sent(send, sendx, stage):
        settle(sendx.at[pl.ds(0, nz - 1)], ex_sem.at[stage])
        settle(send.at[pl.ds(0, nd - 1)], ex_sem.at[stage + 2])

    exchange(send_a, recv_a, sendx_a, recvx_a, 0)
    recv_a[d] = send_a[d]
    recvx_a[z] = sendx_a[z]
    for slot in range(nz, recvx_a.shape[0]):
        recvx_a[slot] = jnp.zeros(recvx_a.shape[1:], BF16)

    for load in loads[7:]:
        load.wait()
    own[...] = dot_tt(cot[:masters], wself[...]) + part[:masters]
    inner_lanes = pick.shape[1] - 128
    lanes = jnp.concatenate(
        [list_lanes(mrow, mcnt, inner_lanes), list_lanes(xrow, xcnt, 128)], axis=1
    )
    master_of = iota(pick.shape, 0).astype(F32)
    pick[...] = one_hot(master_of == lanes).astype(BF16)

    slots_t = jnp.transpose(jnp.broadcast_to(lanes, (128, lanes.shape[1])))
    for block in range(masters // 128):
        columns = slice(block * 128, block * 128 + 128)
        master_at = (iota(slots_t.shape, 1) + block * 128).astype(F32)
        pick_t[:, columns] = one_hot(slots_t == master_at).astype(BF16)

    settle(w_rsin.at[pl.ds(0, chips - 1)], w_recv.at[1])
    w_zin[z] = jnp.sum(w_rsin[...].astype(F32), axis=0).astype(Z_TYPE)

    each_z(lambda there: push(w_zin.at[z], w_zin.at[z], 2, (there, d)))

    arrived(recv_a, recvx_a, 0)
    back = jnp.concatenate([from_chunks(recv_a[...]), from_chunks(recvx_a[...])], axis=0).astype(BF16)
    master[...] = (own[...] + dot_nn(pick[...], back)).astype(BF16)
    copies = dot_nn(pick_t[...], master[...])
    send_b[...] = to_chunks(copies[:inner_lanes])
    sendx_b[...] = to_chunks(copies[inner_lanes:])
    settle(w_zin.at[pl.ds(0, nz - 1)], w_recv.at[2])
    total = w_zin[0].astype(F32)
    for step in range(1, nz):
        total = total + w_zin[step].astype(F32)
    w_ag[chip] = (total * scale).astype(BF16)

    each_chip(lambda there: push(w_ag.at[chip], w_ag.at[chip], 3, (z, there)), False)

    exchange(send_b, recv_b, sendx_b, recvx_b, 4)
    store(master, master_out, 0)
    store(send_b.at[d], recv_b.at[d], 1)
    store(sendx_b.at[z], recvx_b.at[z], 2)

    settle(w_ag.at[pl.ds(0, chips - 1)], w_recv.at[3])
    push(w_ag, w_out.at[core], 4, partner)
    store(w_ag, w_out.at[core], 3)

    arrived(recv_b, recvx_b, 4)
    settle(w_ag, w_recv.at[4])
    for copy in stores:
        copy.wait()

    sent(send_a, sendx_a, 0)
    sent(send_b, sendx_b, 4)
    settle(w_pair, w_send.at[0])
    settle(w_rsin.at[pl.ds(0, chips - 1)], w_send.at[1])
    settle(w_zin.at[pl.ds(0, nz - 1)], w_send.at[2])
    settle(w_ag.at[pl.ds(0, chips - 1)], w_send.at[3])
    settle(w_ag, w_send.at[4])


def finish(
    nz, master_in, recv_in, recvx_in, w_in, slots_out, weights_out,
    master, recv, recvx, parts, slots, weights, in_sem, out_sem,
):
    taken = [
        pltpu.make_async_copy(src, dst, in_sem.at[place])
        for place, (src, dst) in enumerate(
            [(w_in, parts), (recv_in, recv), (master_in, master), (recvx_in, recvx)]
        )
    ]
    for copy in taken:
        copy.start()
    masters, inner = master.shape[0], recv.shape[0] * 8
    inner_end = masters + inner
    given = []

    def give(src, dst):
        copy = pltpu.make_async_copy(src, dst, out_sem.at[len(given)])
        copy.start()
        given.append(copy)

    taken[0].wait()
    for half in range(2):
        weights[half] = from_chunks(parts[half])
        give(weights.at[half], weights_out.at[half])
    taken[1].wait()
    slots[:inner] = from_chunks(recv[...]).astype(BF16)
    give(slots.at[pl.ds(0, inner)], slots_out.at[pl.ds(masters, inner)])
    taken[2].wait()
    give(master, slots_out.at[pl.ds(0, masters)])
    taken[3].wait()
    lists = from_chunks(recvx[...]).astype(BF16)
    tail = slots.shape[0] - inner
    row, column = iota((tail, nz * 8), 0), iota((tail, nz * 8), 1)
    gather = (column // 8 == row // 4) & (column % 8 == row % 4) & (row < nz * 4)
    slots[inner:] = dot_nn(one_hot(gather).astype(BF16), lists).astype(BF16)
    give(slots.at[pl.ds(inner, tail)], slots_out.at[pl.ds(inner_end, tail)])
    for copy in given:
        copy.wait()


def body(
    sizes,
    cotangent, features, aggregated, w_self, w_neigh, edge_tiles,
    tile_rows, tile_cols, mirror_rows, mirror_count, cross_rows, cross_count,
):
    nx, ny, nz = sizes
    nd = nx * ny * 2
    mirror_rows = jnp.swapaxes(mirror_rows, 1, 2)
    cross_rows = jnp.swapaxes(cross_rows, 1, 2)
    slot_count, width = cotangent.shape
    masters = features.shape[0]
    tile_total = edge_tiles.shape[0]
    blocks = slot_count // 128
    scale = 1.0 / math.sqrt(masters * nd * nz)
    grain = width // (nx * ny)
    narrow = (nx * ny, 2 * grain, width // 2)
    hbm = pl.BlockSpec(memory_space=pltpu.HBM)
    lanes = (nd * 8 + 127) // 128 * 128 + 128
    chunk = (16, width // 2)
    dma = pltpu.SemaphoreType.DMA
    outs = (
        jax.ShapeDtypeStruct((slot_count, width), BF16),
        jax.ShapeDtypeStruct((2, width, width), F32),
    )
    landed = (
        jax.ShapeDtypeStruct((masters, width), BF16),
        jax.ShapeDtypeStruct((nd,) + chunk, BF16),
        jax.ShapeDtypeStruct((nz,) + chunk, BF16),
        jax.ShapeDtypeStruct((2,) + narrow, BF16),
    )
    found = pl.pallas_call(
        functools.partial(kernel, sizes, scale),
        out_shape=landed,
        in_specs=[hbm] * 12,
        out_specs=(hbm,) * 4,
        scratch_shapes=[
            pltpu.VMEM(cotangent.shape, BF16),
            pltpu.VMEM(features.shape, BF16),
            pltpu.VMEM(aggregated.shape, BF16),
            pltpu.VMEM(w_self.shape, BF16),
            pltpu.VMEM(w_neigh.shape, BF16),
            pltpu.VMEM(edge_tiles.shape, BF16),
            pltpu.SMEM(tile_rows.shape, jnp.int32),
            pltpu.SMEM(tile_cols.shape, jnp.int32),
            pltpu.VMEM(mirror_rows.shape, jnp.int32),
            pltpu.VMEM(mirror_count.shape, jnp.int32),
            pltpu.VMEM(cross_rows.shape, jnp.int32),
            pltpu.VMEM(cross_count.shape, jnp.int32),
            pltpu.VMEM((blocks, 128, width), BF16),
            pltpu.VMEM((tile_total + 1, 128, width), F32),
            pltpu.VMEM((slot_count, width), F32),
            pltpu.VMEM((masters, width), F32),
            pltpu.VMEM((masters, width), BF16),
            pltpu.VMEM((masters, lanes), BF16),
            pltpu.VMEM((lanes, masters), BF16),
            pltpu.VMEM((nd,) + chunk, BF16),
            pltpu.VMEM((nd,) + chunk, BF16),
            pltpu.VMEM((nd,) + chunk, BF16),
            pltpu.VMEM((16,) + chunk, BF16),
            pltpu.VMEM((16,) + chunk, BF16),
            pltpu.VMEM((16,) + chunk, BF16),
            pltpu.VMEM((2, width, width), F32),
            pltpu.VMEM((width, width), F32),
            pltpu.VMEM(narrow, BF16),
            pltpu.VMEM(narrow, BF16),
            pltpu.VMEM((nz,) + narrow[1:], Z_TYPE),
            pltpu.VMEM(narrow, BF16),
            dma((12,)),
            dma((4,)),
            dma((8,)),
            dma((5,)),
            dma((5,)),
        ],
        compiler_params=pltpu.CompilerParams(
            collective_id=0, has_side_effects=True, vmem_limit_bytes=VMEM_LIMIT
        ),
    )(
        cotangent, features, aggregated, w_self, w_neigh, edge_tiles,
        tile_rows, tile_cols, mirror_rows, mirror_count, cross_rows, cross_count,
    )
    return pl.pallas_call(
        functools.partial(finish, nz),
        out_shape=outs,
        in_specs=[hbm] * 4,
        out_specs=(hbm, hbm),
        scratch_shapes=[pltpu.VMEM(array.shape, array.dtype) for array in landed]
        + [
            pltpu.VMEM((slot_count - masters, width), BF16),
            pltpu.VMEM(outs[1].shape, F32),
            dma((4,)),
            dma((5,)),
        ],
        compiler_params=pltpu.CompilerParams(vmem_limit_bytes=VMEM_LIMIT),
    )(*found)


def solution(mesh, grid=(4, 8)):
    nx, ny = grid
    nz = mesh.shape["grp"]
    both = ("grp", "dom")
    placed = (
        P(both, None), P(both, None), P(both, None), P(), P(), P(both, None, None),
        P(both), P(both), P(both, None, None), P(both, None), P(both, None, None),
        P(both, None),
    )
    return jax.shard_map(
        functools.partial(body, (nx, ny, nz)),
        mesh=mesh, in_specs=placed, out_specs=(P(both, None), P()), check_vma=False,
    )
```

```python
import functools
import math

import jax
import jax.numpy as jnp
from jax import lax
from jax.experimental import pallas as pl
from jax.experimental.pallas import tpu as pltpu
from jax.sharding import PartitionSpec as P

F32 = jnp.float32
BF16 = jnp.bfloat16
MESH = pl.DeviceIdType.MESH
UNROLL = 8
Z_TYPE = F32
VMEM_LIMIT = 60 * 1024 * 1024


def dot_tt(left, right):
    return lax.dot_general(left, right, (((1,), (1,)), ((), ())), preferred_element_type=F32)


def dot_nn(left, right):
    return lax.dot_general(left, right, (((1,), (0,)), ((), ())), preferred_element_type=F32)


def dot_tn(left, right):
    return lax.dot_general(left, right, (((0,), (0,)), ((), ())), preferred_element_type=F32)


def iota(shape, axis):
    return lax.broadcasted_iota(jnp.int32, shape, axis)


def one_hot(mask):
    return jnp.where(mask, 1.0, 0.0).astype(F32)


def list_lanes(rows_ref, count_ref, lanes):
    capacity, peers = rows_ref.shape[1], rows_ref.shape[2]
    mine = iota((peers, lanes), 1) // 8 == iota((peers, lanes), 0)
    spread = lax.dot_general(
        rows_ref[0].astype(F32), one_hot(mine), (((1,), (0,)), ((), ())),
        precision=lax.Precision.HIGHEST, preferred_element_type=F32,
    )
    entry = iota((capacity, lanes), 1) % 8 == iota((capacity, lanes), 0)
    rows = jnp.sum(jnp.where(entry, spread, 0.0), axis=0, keepdims=True)
    counts = lax.dot_general(
        count_ref[...].astype(F32), one_hot(mine), (((1,), (0,)), ((), ())),
        precision=lax.Precision.HIGHEST, preferred_element_type=F32,
    )
    live = (iota((1, lanes), 1) % 8).astype(F32) < counts
    return jnp.where(live, rows, -1.0)


def to_chunks(rows, size=8):
    count, half = rows.shape[0] // size, rows.shape[1] // 2
    left = rows[:, :half].reshape(count, size, half)
    right = rows[:, half:].reshape(count, size, half)
    return jnp.concatenate([left, right], axis=1).astype(BF16)


def from_chunks(chunks):
    count, size, half = chunks.shape[0], chunks.shape[1] // 2, chunks.shape[2]
    wide = chunks.astype(F32)
    left = wide[:, :size].reshape(count * size, half)
    right = wide[:, size:].reshape(count * size, half)
    return jnp.concatenate([left, right], axis=1)


def kernel(
    sizes, scale,
    cot_hbm, feat_hbm, agg_hbm, wself_hbm, wneigh_hbm, tiles_hbm,
    trow_hbm, tcol_hbm, mrow_hbm, mcnt_hbm, xrow_hbm, xcnt_hbm,
    master_out, recv_b, recvx_b, w_out,
    cot, feat, agg, wself, wneigh, tiles, trow, tcol, mrow, mcnt, xrow, xcnt, grads, run, part, own, master,
    pick, pick_t, send_a, recv_a, send_b, sendx_a, recvx_a, sendx_b,
    w_local, w_pair, w_rs, w_rsin, w_zin, w_ag,
    load_sem, store_sem, ex_sem, w_send, w_recv,
):
    nx, ny, nz = sizes
    nd = nx * ny * 2
    masters = feat.shape[0]
    chips = nx * ny
    grain = w_zin.shape[1] // 2
    blocks = grads.shape[0]
    tile_total = tiles.shape[0]
    inner_end = masters + nd * 8
    z = lax.axis_index("grp")
    d = lax.axis_index("dom")
    core = lax.rem(d, 2)
    y = lax.rem(lax.div(d, 2), ny)
    x = lax.div(d, 2 * ny)
    chip = x * ny + y

    def away(place, length):
        return length // 2 + (place + 1) // 2 * (place % 2 * 2 - 1)

    x_ahead = [lax.rem(x + away(step, nx), nx) * ny for step in range(nx)]

    def each_chip(act, with_cores):
        def column(y_there, last):
            for step in range(nx):
                there = (x_ahead[step] + y_there) * 2
                own = last and step == nx - 1
                if with_cores:
                    act(there + 1 - core)
                if not own:
                    act(there + core)

        @pl.loop(0, ny - 1)
        def _(step):
            column(lax.rem(y + away(step, ny), ny), False)

        column(y, True)

    def each_z(act):
        for step in range(nz - 1):
            act(lax.rem(z + away(step, nz), nz))

    barrier = pltpu.get_barrier_semaphore()

    def greet(target):
        pl.semaphore_signal(barrier, inc=1, device_id=target, device_id_type=MESH)

    each_z(lambda there: greet((there, d)))

    loads = [
        pltpu.make_async_copy(src, dst, load_sem.at[place])
        for place, (src, dst) in enumerate(
            [(cot_hbm, cot), (wneigh_hbm, wneigh), (trow_hbm, trow), (tcol_hbm, tcol),
             (tiles_hbm, tiles), (feat_hbm, feat), (agg_hbm, agg), (wself_hbm, wself),
             (mrow_hbm, mrow), (mcnt_hbm, mcnt), (xrow_hbm, xrow), (xcnt_hbm, xcnt)]
        )
    ]
    for load in loads[:2]:
        load.start()
    each_chip(lambda there: greet((z, there)), True)
    for load in loads[2:]:
        load.start()

    def push(src, dst, stage, target):
        copy = pltpu.make_async_remote_copy(
            src_ref=src, dst_ref=dst, send_sem=w_send.at[stage], recv_sem=w_recv.at[stage],
            device_id=target, device_id_type=MESH,
        )
        copy.start()

    stores = []

    def store(src, dst, place):
        copy = pltpu.make_async_copy(src, dst, store_sem.at[place])
        copy.start()
        stores.append(copy)

    def settle(ref, sem):
        pltpu.make_async_copy(ref, ref, sem).wait()

    loads[0].wait()
    loads[1].wait()
    for block in range(blocks):
        rows = slice(block * 128, block * 128 + 128)
        grads[block] = dot_tt(cot[rows], wneigh[...]).astype(BF16)

    run[0] = jnp.zeros(run.shape[1:], F32)
    for load in loads[2:5]:
        load.wait()

    def tile_group(group, last):
        for step in range(UNROLL):
            k = group * UNROLL + step
            column = tcol[k]
            before = last[0]
            for block in range(1, blocks):
                before = jnp.where(column == block, last[block], before)
            product = dot_tn(tiles[k], grads[trow[k]])
            run[k + 1] = product + run[before]
            last = tuple(
                jnp.where(column == block, k + 1, last[block]) for block in range(blocks)
            )
        return last

    groups = tile_total // UNROLL
    last = tuple(jnp.int32(0) for _ in range(blocks))
    last = lax.fori_loop(0, groups // 2, tile_group, last)

    loads[5].wait()
    w_local[0] = dot_tn(feat[...], cot[:masters])
    loads[6].wait()
    w_local[1] = dot_tn(agg[...], cot[:masters])

    pl.semaphore_wait(barrier, nd - 1 + nz - 1)
    partner = (z, d + 1 - 2 * core)
    push(w_local.at[1 - core], w_pair, 0, partner)

    last = lax.fori_loop(groups // 2, groups, tile_group, last)
    for block in range(blocks):
        part[block * 128:block * 128 + 128] = run[last[block]]


    send_a[...] = to_chunks(part[masters:inner_end])
    spread = (iota((128, 128), 0) // 8 == iota((128, 128), 1) // 4) & (
        iota((128, 128), 0) % 8 == iota((128, 128), 1) % 4
    ) & (iota((128, 128), 1) < nz * 4)
    sendx_a[...] = to_chunks(
        dot_nn(one_hot(spread).astype(BF16), part[inner_end:inner_end + 128].astype(BF16))
    )

    settle(w_pair, w_recv.at[0])
    w_rs[...] = to_chunks(w_local[core] + w_pair[...], grain)

    each_chip(
        lambda there: push(w_rs.at[lax.div(there, 2)], w_rsin.at[chip], 1, (z, there)), False
    )

    w_rsin[chip] = w_rs[chip]
    def exchange(send, recv, sendx, recvx, stage):
        def to_peer(target):
            pltpu.make_async_remote_copy(
                src_ref=send.at[target], dst_ref=recv.at[d],
                send_sem=ex_sem.at[stage + 2], recv_sem=ex_sem.at[stage + 3],
                device_id=(z, target), device_id_type=MESH,
            ).start()

        def to_group(target):
            pltpu.make_async_remote_copy(
                src_ref=sendx.at[target], dst_ref=recvx.at[z],
                send_sem=ex_sem.at[stage], recv_sem=ex_sem.at[stage + 1],
                device_id=(target, d), device_id_type=MESH,
            ).start()

        each_chip(to_peer, True)
        each_z(to_group)

    def arrived(recv, recvx, stage):
        settle(recvx.at[pl.ds(0, nz - 1)], ex_sem.at[stage + 1])
        settle(recv.at[pl.ds(0, nd - 1)], ex_sem.at[stage + 3])

    def sent(send, sendx, stage):
        settle(sendx.at[pl.ds(0, nz - 1)], ex_sem.at[stage])
        settle(send.at[pl.ds(0, nd - 1)], ex_sem.at[stage + 2])

    exchange(send_a, recv_a, sendx_a, recvx_a, 0)
    recv_a[d] = send_a[d]
    recvx_a[z] = sendx_a[z]
    for slot in range(nz, recvx_a.shape[0]):
        recvx_a[slot] = jnp.zeros(recvx_a.shape[1:], BF16)

    for load in loads[7:]:
        load.wait()
    own[...] = dot_tt(cot[:masters], wself[...]) + part[:masters]
    inner_lanes = pick.shape[1] - 128
    lanes = jnp.concatenate(
        [list_lanes(mrow, mcnt, inner_lanes), list_lanes(xrow, xcnt, 128)], axis=1
    )
    master_of = iota(pick.shape, 0).astype(F32)
    pick[...] = one_hot(master_of == lanes).astype(BF16)

    slots_t = jnp.transpose(jnp.broadcast_to(lanes, (128, lanes.shape[1])))
    for block in range(masters // 128):
        columns = slice(block * 128, block * 128 + 128)
        master_at = (iota(slots_t.shape, 1) + block * 128).astype(F32)
        pick_t[:, columns] = one_hot(slots_t == master_at).astype(BF16)

    settle(w_rsin.at[pl.ds(0, chips - 1)], w_recv.at[1])
    w_zin[z] = jnp.sum(w_rsin[...].astype(F32), axis=0).astype(Z_TYPE)

    each_z(lambda there: push(w_zin.at[z], w_zin.at[z], 2, (there, d)))

    arrived(recv_a, recvx_a, 0)
    back = jnp.concatenate([from_chunks(recv_a[...]), from_chunks(recvx_a[...])], axis=0).astype(BF16)
    master[...] = (own[...] + dot_nn(pick[...], back)).astype(BF16)
    copies = dot_nn(pick_t[...], master[...])
    send_b[...] = to_chunks(copies[:inner_lanes])
    sendx_b[...] = to_chunks(copies[inner_lanes:])
    settle(w_zin.at[pl.ds(0, nz - 1)], w_recv.at[2])
    total = w_zin[0].astype(F32)
    for step in range(1, nz):
        total = total + w_zin[step].astype(F32)
    w_ag[chip] = (total * scale).astype(BF16)

    each_chip(lambda there: push(w_ag.at[chip], w_ag.at[chip], 3, (z, there)), False)

    exchange(send_b, recv_b, sendx_b, recvx_b, 4)
    store(master, master_out, 0)
    store(send_b.at[d], recv_b.at[d], 1)
    store(sendx_b.at[z], recvx_b.at[z], 2)

    settle(w_ag.at[pl.ds(0, chips - 1)], w_recv.at[3])
    push(w_ag, w_out.at[core], 4, partner)
    store(w_ag, w_out.at[core], 3)

    arrived(recv_b, recvx_b, 4)
    settle(w_ag, w_recv.at[4])
    for copy in stores:
        copy.wait()

    sent(send_a, sendx_a, 0)
    sent(send_b, sendx_b, 4)
    settle(w_pair, w_send.at[0])
    settle(w_rsin.at[pl.ds(0, chips - 1)], w_send.at[1])
    settle(w_zin.at[pl.ds(0, nz - 1)], w_send.at[2])
    settle(w_ag.at[pl.ds(0, chips - 1)], w_send.at[3])
    settle(w_ag, w_send.at[4])


def finish(
    nz, master_in, recv_in, recvx_in, w_in, slots_out, weights_out,
    master, recv, recvx, parts, slots, weights, in_sem, out_sem,
):
    taken = [
        pltpu.make_async_copy(src, dst, in_sem.at[place])
        for place, (src, dst) in enumerate(
            [(w_in, parts), (recv_in, recv), (master_in, master), (recvx_in, recvx)]
        )
    ]
    for copy in taken:
        copy.start()
    masters, inner = master.shape[0], recv.shape[0] * 8
    inner_end = masters + inner
    given = []

    def give(src, dst):
        copy = pltpu.make_async_copy(src, dst, out_sem.at[len(given)])
        copy.start()
        given.append(copy)

    taken[0].wait()
    for half in range(2):
        weights[half] = from_chunks(parts[half])
        give(weights.at[half], weights_out.at[half])
    taken[1].wait()
    slots[:inner] = from_chunks(recv[...]).astype(BF16)
    give(slots.at[pl.ds(0, inner)], slots_out.at[pl.ds(masters, inner)])
    taken[2].wait()
    give(master, slots_out.at[pl.ds(0, masters)])
    taken[3].wait()
    lists = from_chunks(recvx[...]).astype(BF16)
    tail = slots.shape[0] - inner
    row, column = iota((tail, nz * 8), 0), iota((tail, nz * 8), 1)
    gather = (column // 8 == row // 4) & (column % 8 == row % 4) & (row < nz * 4)
    slots[inner:] = dot_nn(one_hot(gather).astype(BF16), lists).astype(BF16)
    give(slots.at[pl.ds(inner, tail)], slots_out.at[pl.ds(inner_end, tail)])
    for copy in given:
        copy.wait()


def body(
    sizes,
    cotangent, features, aggregated, w_self, w_neigh, edge_tiles,
    tile_rows, tile_cols, mirror_rows, mirror_count, cross_rows, cross_count,
):
    nx, ny, nz = sizes
    nd = nx * ny * 2
    mirror_rows = jnp.swapaxes(mirror_rows, 1, 2)
    cross_rows = jnp.swapaxes(cross_rows, 1, 2)
    slot_count, width = cotangent.shape
    masters = features.shape[0]
    tile_total = edge_tiles.shape[0]
    blocks = slot_count // 128
    scale = 1.0 / math.sqrt(masters * nd * nz)
    grain = width // (nx * ny)
    narrow = (nx * ny, 2 * grain, width // 2)
    hbm = pl.BlockSpec(memory_space=pltpu.HBM)
    lanes = (nd * 8 + 127) // 128 * 128 + 128
    chunk = (16, width // 2)
    dma = pltpu.SemaphoreType.DMA
    outs = (
        jax.ShapeDtypeStruct((slot_count, width), BF16),
        jax.ShapeDtypeStruct((2, width, width), F32),
    )
    landed = (
        jax.ShapeDtypeStruct((masters, width), BF16),
        jax.ShapeDtypeStruct((nd,) + chunk, BF16),
        jax.ShapeDtypeStruct((nz,) + chunk, BF16),
        jax.ShapeDtypeStruct((2,) + narrow, BF16),
    )
    found = pl.pallas_call(
        functools.partial(kernel, sizes, scale),
        out_shape=landed,
        in_specs=[hbm] * 12,
        out_specs=(hbm,) * 4,
        scratch_shapes=[
            pltpu.VMEM(cotangent.shape, BF16),
            pltpu.VMEM(features.shape, BF16),
            pltpu.VMEM(aggregated.shape, BF16),
            pltpu.VMEM(w_self.shape, BF16),
            pltpu.VMEM(w_neigh.shape, BF16),
            pltpu.VMEM(edge_tiles.shape, BF16),
            pltpu.SMEM(tile_rows.shape, jnp.int32),
            pltpu.SMEM(tile_cols.shape, jnp.int32),
            pltpu.VMEM(mirror_rows.shape, jnp.int32),
            pltpu.VMEM(mirror_count.shape, jnp.int32),
            pltpu.VMEM(cross_rows.shape, jnp.int32),
            pltpu.VMEM(cross_count.shape, jnp.int32),
            pltpu.VMEM((blocks, 128, width), BF16),
            pltpu.VMEM((tile_total + 1, 128, width), F32),
            pltpu.VMEM((slot_count, width), F32),
            pltpu.VMEM((masters, width), F32),
            pltpu.VMEM((masters, width), BF16),
            pltpu.VMEM((masters, lanes), BF16),
            pltpu.VMEM((lanes, masters), BF16),
            pltpu.VMEM((nd,) + chunk, BF16),
            pltpu.VMEM((nd,) + chunk, BF16),
            pltpu.VMEM((nd,) + chunk, BF16),
            pltpu.VMEM((16,) + chunk, BF16),
            pltpu.VMEM((16,) + chunk, BF16),
            pltpu.VMEM((16,) + chunk, BF16),
            pltpu.VMEM((2, width, width), F32),
            pltpu.VMEM((width, width), F32),
            pltpu.VMEM(narrow, BF16),
            pltpu.VMEM(narrow, BF16),
            pltpu.VMEM((nz,) + narrow[1:], Z_TYPE),
            pltpu.VMEM(narrow, BF16),
            dma((12,)),
            dma((4,)),
            dma((8,)),
            dma((5,)),
            dma((5,)),
        ],
        compiler_params=pltpu.CompilerParams(
            collective_id=0, has_side_effects=True, vmem_limit_bytes=VMEM_LIMIT
        ),
    )(
        cotangent, features, aggregated, w_self, w_neigh, edge_tiles,
        tile_rows, tile_cols, mirror_rows, mirror_count, cross_rows, cross_count,
    )
    return pl.pallas_call(
        functools.partial(finish, nz),
        out_shape=outs,
        in_specs=[hbm] * 4,
        out_specs=(hbm, hbm),
        scratch_shapes=[pltpu.VMEM(array.shape, array.dtype) for array in landed]
        + [
            pltpu.VMEM((slot_count - masters, width), BF16),
            pltpu.VMEM(outs[1].shape, F32),
            dma((4,)),
            dma((5,)),
        ],
        compiler_params=pltpu.CompilerParams(vmem_limit_bytes=VMEM_LIMIT),
    )(*found)


def solution(mesh, grid=(4, 8)):
    nx, ny = grid
    nz = mesh.shape["grp"]
    both = ("grp", "dom")
    placed = (
        P(both, None), P(both, None), P(both, None), P(), P(), P(both, None, None),
        P(both), P(both), P(both, None, None), P(both, None), P(both, None, None),
        P(both, None),
    )
    return jax.shard_map(
        functools.partial(body, (nx, ny, nz)),
        mesh=mesh, in_specs=placed, out_specs=(P(both, None), P()), check_vma=False,
    )
```
